32 devices in a mesh: dp: 4 (over x, core), mp: 8 (over z, y).
Axes of the slice: x: 2, y: 2, z: 4, core: 2. Of those that a mesh axis runs over, the one named last changes fastest.
Arguments:
- hidden: bfloat16 [2048, 4096], P('dp'), may hold values from -170 to 170
- encoded: bfloat16 [32, 114688], P('dp'), may hold values from -4 to 4
- neighbours: int32 [32, 2], P('dp'), may hold values from 0 to 31, as said below
- w_query: bfloat16 [4096, 4096], P(None, 'mp'), as said below
- w_key: bfloat16 [896, 4096], P(None, 'mp'), as said below
- w_value: bfloat16 [896, 4096], P(None, 'mp'), may hold values from -0.1875 to 0.1875
- w_out: bfloat16 [4096, 4096], P('mp'), may hold values from -0.125 to 0.125
- cotangent: bfloat16 [2048, 4096], P('dp'), may hold values from -16 to 16
Outputs:
- attended: bfloat16 [2048, 4096], P('dp', 'mp')
- grad_hidden: bfloat16 [2048, 4096], P('dp', 'mp')
- grad_encoded: bfloat16 [32, 114688], P('dp', 'mp')
The draws below stay inside these ranges and needn't reach their ends.
Inputs may be any that keep to these rules, and one draw needn't show every extreme that they name: `neighbours`: an id is owner * 8 + slot: the neighbour is row slot of the rows of encoded held by dp index owner. Of the 16 ids of one index of dp, at most 4 name one owner; one owner, the same for every index, is named exactly 4 times by every index of dp. `w_query`: entries scaled by the inverse square root of 4096. `w_key`: entries scaled by the inverse square root of 896, or smaller.
All inputs are finite; a program needn't handle non-finite values.
Results may differ from the reference program's by a relative error of at most 0.0065.
The reference program's roundings to bfloat16 on the way (of `queries`, `prob_half`, `attn_out`, `grad_attn`, `grad_values` and `grad_scores`) count: a program that leaves them out, or rounds other values in their place, can miss the bound.
Values may be sent and summed in bfloat16 or wider, within the bound.
A program may use at most 128 MiB of HBM per device.

```python
import math
import jax
import jax.numpy as jnp
from jax import lax

D = 4096
HEADS = 32
DH = 128
DE = 896
CL = 64
LN = 128
NEIGH = 2
NB_DEV = 8
CH_DEV = 8
CAP = 4
TOKENS = 2048
SPANS = 32
NB = 32


def encoded_base(key):
    key_a = jax.random.fold_in(jax.random.fold_in(key, 101), 0)
    values = jnp.clip(jax.random.normal(key_a, (NB, LN, DE), jnp.float32), -4.0, 4.0)
    return values


def neighbour_base(key):
    key_a, key_b, key_c, key_d, key_e, key_f = jax.random.split(jax.random.fold_in(key, 202), 6)
    owners = NB // NB_DEV
    requests = NEIGH * CH_DEV
    hot_owner = jax.random.randint(key_a, (), 0, owners)
    position = jnp.arange(requests)
    pattern = jnp.where(position < CAP, 0, 1 + (position - CAP) % (owners - 1))
    sub_keys = jax.random.split(key_b, owners)
    order = jax.vmap(lambda sub_key: jax.random.permutation(sub_key, requests))(sub_keys)
    owner_idx = (hot_owner + pattern[order]) % owners
    favourite = jax.random.randint(key_c, (4,), 0, NB_DEV)
    use_favourite = jax.random.randint(key_d, (owners, requests), 0, 2)
    favoured = favourite[jax.random.randint(key_e, (owners, requests), 0, 4)]
    slots = jnp.where(use_favourite == 0, favoured, jax.random.randint(key_f, (owners, requests), 0, NB_DEV))
    return (owner_idx * NB_DEV + slots).reshape(SPANS, NEIGH).astype(jnp.int32)


def query_base(key):
    key_a = jax.random.fold_in(key, 404)
    values = jnp.clip(jax.random.normal(key_a, (D, D), jnp.float32), -4.0, 4.0)
    return values / math.sqrt(D)


def draw_hidden(key, part):
    key_a = jax.random.fold_in(jax.random.fold_in(key, 303), 0)
    values = jnp.clip(2.0 * jax.random.normal(key_a, (TOKENS, D), jnp.float32), -8.0, 8.0)
    return values.astype(jnp.bfloat16)


def draw_encoded(key, part):
    return encoded_base(key).reshape(NB, LN * DE).astype(jnp.bfloat16)


def draw_neighbours(key, part):
    return neighbour_base(key)


def draw_w_query(key, part):
    return query_base(key).astype(jnp.bfloat16)


def draw_w_key(key, part):
    values = jnp.clip(jax.random.normal(jax.random.fold_in(key, 505), (DE, D), jnp.float32), -4.0, 4.0) / math.sqrt(DE)
    return values.astype(jnp.bfloat16)


def with_spikes(values, stream_key, source, target, blocks, factor):
    def block_of(axis_at):
        return (jnp.arange(values.shape[axis_at]) // (values.shape[axis_at] // blocks)).reshape((-1,) + (1,) * (values.ndim - 1 - axis_at))

    first = jax.random.permutation(stream_key, blocks)[block_of(target)]
    other_side = (block_of(target) + blocks // 2) % blocks
    return jnp.where((block_of(source) == first) | (block_of(source) == other_side), factor * values, values)


def shard_levels(rng, dims, shards, smallest, high):
    def one(dim, shards_of):
        heights = jax.random.uniform(jax.random.fold_in(jax.random.fold_in(rng, 6), dim), (shards_of,), jnp.float32, smallest / len(shards), high / len(shards))
        return jnp.repeat(jnp.exp(heights), dims[dim] // shards_of).reshape((-1,) + (1,) * (len(dims) - dim - 1))

    loudness = one(*shards[0])
    for cut in shards[1:]:
        loudness = loudness * one(*cut)
    return loudness


def bell_draw(key, extent, width, reach, cuts=(), dtype=jnp.bfloat16):
    gain = shard_levels(key, extent, cuts, -0.22, 0.18) if cuts else 1.0
    drawn = jax.random.normal(key, extent, jnp.float32) * width * gain
    return jnp.minimum(jnp.maximum(drawn, -reach), reach).astype(dtype)


def gaussian_with(rng, dims, deviation, reach, pieces, heavy, held_as=jnp.bfloat16):
    values = deviation * jax.random.normal(rng, dims, jnp.float32)
    if pieces:
        values = values * shard_levels(rng, dims, pieces, -0.22, 0.18)
    return jnp.clip(with_spikes(values, jax.random.fold_in(rng, 3), *heavy), -reach, reach).astype(held_as)


def setup_inputs(seed: int = 0) -> dict:
    key_of = jax.random.split(jax.random.key(seed), 9)
    hidden = draw_hidden(jax.random.fold_in(key_of[8], 71), 0)
    encoded = draw_encoded(jax.random.fold_in(key_of[8], 71), 0)
    neighbours = draw_neighbours(jax.random.fold_in(key_of[8], 71), 0)
    w_query = draw_w_query(jax.random.fold_in(key_of[8], 71), 0)
    w_key = draw_w_key(jax.random.fold_in(key_of[8], 71), 0)
    w_value = bell_draw(key_of[5], (DE, D), DE ** -0.5, 0.1875, ((1, 8),))
    w_out = gaussian_with(key_of[6], (D, D), D ** -0.5, 0.125, ((0, 8),), (0, 1, 8, 2.0))
    cotangent = bell_draw(key_of[7], (TOKENS, D), 4.0, 16.0, ((0, 4),))
    return dict(hidden=hidden, encoded=encoded, neighbours=neighbours, w_query=w_query, w_key=w_key, w_value=w_value, w_out=w_out, cotangent=cotangent)


def to_half(value):
    return lax.optimization_barrier(value.astype(jnp.bfloat16))

def reference(hidden, encoded, neighbours, w_query, w_key, w_value, w_out, cotangent):
    inv_root = 1.0 / math.sqrt(DH)
    enc_rows = encoded.reshape(NB * LN, DE)
    flat_ids = neighbours.reshape(SPANS * NEIGH).astype(jnp.int32)
    query_heads = w_query.reshape(D, HEADS, DH).transpose(1, 0, 2)
    key_heads = w_key.reshape(DE, HEADS, DH).transpose(1, 0, 2)
    value_heads = w_value.reshape(DE, HEADS, DH).transpose(1, 0, 2)
    out_heads = w_out.reshape(HEADS, DH, D)

    def head_step(carry, parts):
        att_acc, hid_acc, enc_acc = carry
        query_w, key_w, value_w, out_w = parts
        queries = to_half(jnp.dot(hidden, query_w, preferred_element_type=jnp.float32))
        keys_all = to_half(jnp.dot(enc_rows, key_w, preferred_element_type=jnp.float32)).reshape(NB, LN, DH)
        values_all = to_half(jnp.dot(enc_rows, value_w, preferred_element_type=jnp.float32)).reshape(NB, LN, DH)
        ctx_keys = jnp.take(keys_all, flat_ids, axis=0).reshape(SPANS, NEIGH * LN, DH).astype(jnp.float32)
        ctx_values = jnp.take(values_all, flat_ids, axis=0).reshape(SPANS, NEIGH * LN, DH).astype(jnp.float32)
        q_blocks = queries.reshape(SPANS, CL, DH).astype(jnp.float32)
        scores = jnp.einsum('cqd,ckd->cqk', q_blocks, ctx_keys) * inv_root
        row_max = lax.optimization_barrier(jnp.max(scores, axis=-1, keepdims=True))
        exp_terms = jnp.exp(scores - row_max)
        prob_full = exp_terms / lax.optimization_barrier(jnp.sum(exp_terms, axis=-1, keepdims=True))
        prob_half = to_half(prob_full).astype(jnp.float32)
        attn_out = to_half(jnp.einsum('cqk,ckd->cqd', prob_half, ctx_values)).reshape(TOKENS, DH)
        att_acc = att_acc + jnp.dot(attn_out, out_w, preferred_element_type=jnp.float32)
        grad_attn = to_half(jnp.dot(cotangent, out_w.T, preferred_element_type=jnp.float32))
        grad_blocks = grad_attn.reshape(SPANS, CL, DH).astype(jnp.float32)
        grad_prob = jnp.einsum('cqd,ckd->cqk', grad_blocks, ctx_values)
        grad_values = to_half(jnp.einsum('cqk,cqd->ckd', prob_half, grad_blocks)).astype(jnp.float32)
        grad_scores = to_half(prob_full * (grad_prob - lax.optimization_barrier(jnp.sum(prob_full * grad_prob, axis=-1, keepdims=True)))).astype(jnp.float32)
        grad_query = to_half(jnp.einsum('cqk,ckd->cqd', grad_scores, ctx_keys) * inv_root).reshape(TOKENS, DH)
        grad_keys = to_half(jnp.einsum('cqk,cqd->ckd', grad_scores, q_blocks) * inv_root).astype(jnp.float32)
        hid_acc = hid_acc + jnp.dot(grad_query, query_w.T, preferred_element_type=jnp.float32)
        key_sum = jnp.zeros((NB, LN, DH), jnp.float32).at[flat_ids].add(grad_keys.reshape(SPANS * NEIGH, LN, DH))
        value_sum = jnp.zeros((NB, LN, DH), jnp.float32).at[flat_ids].add(grad_values.reshape(SPANS * NEIGH, LN, DH))
        key_half = key_sum.astype(jnp.bfloat16).reshape(NB * LN, DH)
        value_half = value_sum.astype(jnp.bfloat16).reshape(NB * LN, DH)
        enc_acc = enc_acc + jnp.dot(key_half, key_w.T, preferred_element_type=jnp.float32)
        enc_acc = enc_acc + jnp.dot(value_half, value_w.T, preferred_element_type=jnp.float32)
        return ((att_acc, hid_acc, enc_acc), None)
    start = (jnp.zeros((TOKENS, D), jnp.float32), jnp.zeros((TOKENS, D), jnp.float32), jnp.zeros((NB * LN, DE), jnp.float32))
    (att_acc, hid_acc, enc_acc), unused = lax.scan(head_step, start, (query_heads, key_heads, value_heads, out_heads))
    attended = att_acc.astype(jnp.bfloat16)
    grad_hidden = hid_acc.astype(jnp.bfloat16)
    grad_encoded = enc_acc.reshape(NB, LN * DE).astype(jnp.bfloat16)
    return (attended, grad_hidden, grad_encoded)
```

```python
import functools
import math

import jax
import jax.numpy as jnp
from jax import lax
from jax.experimental import pallas as pl
from jax.experimental.pallas import tpu as pltpu
from jax.sharding import PartitionSpec as P

DH = 128
VMEM_BYTES = 48 * 1024 * 1024


def dot(a, b, contract):
    return lax.dot_general(a, b, ((contract[:1], contract[1:]), ((), ())), preferred_element_type=jnp.float32)


def attention_kernel(per_block, ids, target, q_ref, ga_ref, *refs):
    kv_refs = refs[:per_block]
    attn_ref, gq_ref, out_ref = refs[per_block:]
    step = pl.program_id(0)
    cols = q_ref.shape[1]
    seg = kv_refs[0].shape[1]
    inv_root = 1.0 / math.sqrt(DH)

    if out_ref.shape[0] > target.shape[0]:
        @pl.when(step == 0)
        def _():
            out_ref[...] = jnp.zeros_like(out_ref)

    for h in range(cols // DH):
        at = h * DH
        q = q_ref[:, at:at + DH]
        ga = ga_ref[:, at:at + DH]
        k = jnp.concatenate([r[0, :, at:at + DH] for r in kv_refs], axis=0)
        v = jnp.concatenate([r[0, :, cols + at:cols + at + DH] for r in kv_refs], axis=0)
        scores = dot(q, k, (1, 1)) * inv_root
        grad_prob = dot(ga, v, (1, 1))
        terms = jnp.exp(scores - jnp.max(scores, axis=-1, keepdims=True))
        prob = terms / jnp.sum(terms, axis=-1, keepdims=True)
        half = prob.astype(jnp.bfloat16)
        attn_ref[:, at:at + DH] = dot(half, v, (1, 0)).astype(jnp.bfloat16)
        grad_v = dot(half, ga, (0, 0)).astype(jnp.bfloat16)
        gs = (prob * (grad_prob - jnp.sum(prob * grad_prob, axis=-1, keepdims=True))).astype(jnp.bfloat16)
        gq_ref[:, at:at + DH] = (dot(gs, k, (1, 0)) * inv_root).astype(jnp.bfloat16)
        grad_k = (dot(gs, q, (0, 0)) * inv_root).astype(jnp.bfloat16)
        for j in range(per_block):
            slot = target[step * per_block + j]
            out_ref[slot, :, at:at + DH] = grad_k[j * seg:(j + 1) * seg]
            out_ref[slot, :, cols + at:cols + at + DH] = grad_v[j * seg:(j + 1) * seg]


def attention(ids, target, queries, grad_attn, kv, blocks, slots):
    per_block = ids.shape[0] // blocks
    tok, cols = queries.shape
    block_len = tok // blocks
    seg = kv.shape[1]
    row = pl.BlockSpec((block_len, cols), lambda c, ids, tg: (c, 0))

    def kv_spec(j):
        return pl.BlockSpec((1, seg, 2 * cols), lambda c, ids, tg: (ids[c * per_block + j], 0, 0))

    return pl.pallas_call(
        functools.partial(attention_kernel, per_block),
        grid_spec=pltpu.PrefetchScalarGridSpec(
            num_scalar_prefetch=2,
            grid=(blocks,),
            in_specs=[row, row] + [kv_spec(j) for j in range(per_block)],
            out_specs=[row, row, pl.BlockSpec((slots, seg, 2 * cols), lambda c, ids, tg: (0, 0, 0))],
        ),
        out_shape=[
            jax.ShapeDtypeStruct((tok, cols), jnp.bfloat16),
            jax.ShapeDtypeStruct((tok, cols), jnp.bfloat16),
            jax.ShapeDtypeStruct((slots, seg, 2 * cols), jnp.bfloat16),
        ],
        compiler_params=pltpu.CompilerParams(vmem_limit_bytes=VMEM_BYTES),
        name="attention",
    )(ids, target, queries, grad_attn, *([kv] * per_block))


def sum_kernel(count, ids, ret_ref, out_ref, acc):
    acc[...] = jnp.zeros_like(acc)

    @pl.loop(0, count)
    def _(i):
        slot = ids[i]

        @pl.when(slot >= 0)
        def _():
            acc[slot] = acc[slot] + ret_ref[i].astype(jnp.float32)

    out_ref[...] = acc[...].astype(jnp.bfloat16)


def sum_slots(ids, returned, stored):
    shape = (stored,) + returned.shape[1:]
    return pl.pallas_call(
        functools.partial(sum_kernel, returned.shape[0]),
        grid_spec=pltpu.PrefetchScalarGridSpec(
            num_scalar_prefetch=1,
            grid=(1,),
            in_specs=[pl.BlockSpec(returned.shape, lambda i, ids: (0, 0, 0))],
            out_specs=pl.BlockSpec(shape, lambda i, ids: (0, 0, 0)),
            scratch_shapes=[pltpu.VMEM(shape, jnp.float32)],
        ),
        out_shape=jax.ShapeDtypeStruct(shape, jnp.bfloat16),
        compiler_params=pltpu.CompilerParams(vmem_limit_bytes=VMEM_BYTES),
        name="sum_slots",
    )(ids, returned)


def shards(hidden, encoded, neighbours, w_query, w_key, w_value, w_out, cotangent):
    owners = lax.axis_size("dp")
    me = lax.axis_index("dp")
    blocks, per_block = neighbours.shape
    requests = blocks * per_block
    capacity = requests // 4
    stored = encoded.shape[0]
    enc_width, head_cols = w_key.shape
    seg_len = encoded.shape[1] // enc_width

    w_pair = jnp.concatenate([w_key, w_value], axis=1)
    enc_rows = encoded.reshape(stored * seg_len, enc_width)
    kv_own = jnp.dot(enc_rows, w_pair, preferred_element_type=jnp.float32).astype(jnp.bfloat16)
    kv = lax.all_gather(kv_own.reshape(stored, seg_len, 2 * head_cols), "dp", axis=0, tiled=True)
    queries = jnp.dot(hidden, w_query, preferred_element_type=jnp.float32).astype(jnp.bfloat16)
    grad_attn = dot(cotangent, w_out, (1, 1)).astype(jnp.bfloat16)

    ids = lax.all_gather(neighbours.reshape(requests), "dp", axis=0)
    owner_of = ids // stored
    slot_of = ids % stored
    same = owner_of[:, :, None] == owner_of[:, None, :]
    before = jnp.arange(requests)[:, None] > jnp.arange(requests)[None, :]
    position = jnp.sum((same & before[None]).astype(jnp.int32), axis=2)
    wanted = (owner_of == me)[:, :, None] & (position[:, :, None] == jnp.arange(capacity)[None, None, :])
    my_slots = (jnp.sum(jnp.where(wanted, slot_of[:, :, None] + 1, 0), axis=1) - 1).reshape(owners * capacity)
    flat_ids = neighbours.reshape(requests)
    flat_owner = flat_ids // stored
    mine = flat_owner[:, None] == flat_owner[None, :]
    target = flat_owner * capacity + jnp.sum((mine & before).astype(jnp.int32), axis=1)

    attn, grad_query, outgoing = attention(
        flat_ids, target, queries, grad_attn, kv, blocks, owners * capacity
    )
    returned = lax.all_to_all(outgoing, "dp", split_axis=0, concat_axis=0, tiled=True)
    partial_value = jnp.dot(attn, w_out, preferred_element_type=jnp.float32).astype(jnp.bfloat16)
    attended = lax.psum_scatter(partial_value, "mp", scatter_dimension=1, tiled=True)
    grad_terms = dot(grad_query, w_query, (1, 1)).astype(jnp.bfloat16)
    grad_hidden = lax.psum_scatter(grad_terms, "mp", scatter_dimension=1, tiled=True)
    grad_stored = sum_slots(my_slots, returned, stored)
    enc_terms = dot(grad_stored.reshape(stored * seg_len, 2 * head_cols), w_pair, (1, 1))
    enc_terms = enc_terms.astype(jnp.bfloat16).reshape(stored, seg_len, enc_width)
    grad_encoded = lax.psum_scatter(enc_terms, "mp", scatter_dimension=1, tiled=True)
    return attended, grad_hidden, grad_encoded.reshape(stored, -1)


def solution(mesh):
    placed = (
        P("dp", None),
        P("dp", None),
        P("dp", None),
        P(None, "mp"),
        P(None, "mp"),
        P(None, "mp"),
        P("mp", None),
        P("dp", None),
    )
    return jax.shard_map(
        shards,
        mesh=mesh,
        in_specs=placed,
        out_specs=(P("dp", "mp"), P("dp", "mp"), P("dp", "mp")),
        check_vma=False,
    )
```

```python
import functools
import math

import jax
import jax.numpy as jnp
from jax import lax
from jax.experimental import pallas as pl
from jax.experimental.pallas import tpu as pltpu
from jax.sharding import PartitionSpec as P

DH = 128
VMEM_BYTES = 48 * 1024 * 1024


def dot(a, b, contract):
    return lax.dot_general(a, b, ((contract[:1], contract[1:]), ((), ())), preferred_element_type=jnp.float32)


def attention_kernel(per_block, ids, target, q_ref, ga_ref, *refs):
    kv_refs = refs[:per_block]
    attn_ref, gq_ref, out_ref = refs[per_block:]
    step = pl.program_id(0)
    cols = q_ref.shape[1]
    seg = kv_refs[0].shape[1]
    inv_root = 1.0 / math.sqrt(DH)

    if out_ref.shape[0] > target.shape[0]:
        @pl.when(step == 0)
        def _():
            out_ref[...] = jnp.zeros_like(out_ref)

    for h in range(cols // DH):
        at = h * DH
        q = q_ref[:, at:at + DH]
        ga = ga_ref[:, at:at + DH]
        k = jnp.concatenate([r[0, :, at:at + DH] for r in kv_refs], axis=0)
        v = jnp.concatenate([r[0, :, cols + at:cols + at + DH] for r in kv_refs], axis=0)
        scores = dot(q, k, (1, 1)) * inv_root
        grad_prob = dot(ga, v, (1, 1))
        terms = jnp.exp(scores - jnp.max(scores, axis=-1, keepdims=True))
        prob = terms / jnp.sum(terms, axis=-1, keepdims=True)
        half = prob.astype(jnp.bfloat16)
        attn_ref[:, at:at + DH] = dot(half, v, (1, 0)).astype(jnp.bfloat16)
        grad_v = dot(half, ga, (0, 0)).astype(jnp.bfloat16)
        gs = (prob * (grad_prob - jnp.sum(prob * grad_prob, axis=-1, keepdims=True))).astype(jnp.bfloat16)
        gq_ref[:, at:at + DH] = (dot(gs, k, (1, 0)) * inv_root).astype(jnp.bfloat16)
        grad_k = (dot(gs, q, (0, 0)) * inv_root).astype(jnp.bfloat16)
        for j in range(per_block):
            slot = target[step * per_block + j]
            out_ref[slot, :, at:at + DH] = grad_k[j * seg:(j + 1) * seg]
            out_ref[slot, :, cols + at:cols + at + DH] = grad_v[j * seg:(j + 1) * seg]


def attention(ids, target, queries, grad_attn, kv, blocks, slots):
    per_block = ids.shape[0] // blocks
    tok, cols = queries.shape
    block_len = tok // blocks
    seg = kv.shape[1]
    row = pl.BlockSpec((block_len, cols), lambda c, ids, tg: (c, 0))

    def kv_spec(j):
        return pl.BlockSpec((1, seg, 2 * cols), lambda c, ids, tg: (ids[c * per_block + j], 0, 0))

    return pl.pallas_call(
        functools.partial(attention_kernel, per_block),
        grid_spec=pltpu.PrefetchScalarGridSpec(
            num_scalar_prefetch=2,
            grid=(blocks,),
            in_specs=[row, row] + [kv_spec(j) for j in range(per_block)],
            out_specs=[row, row, pl.BlockSpec((slots, seg, 2 * cols), lambda c, ids, tg: (0, 0, 0))],
        ),
        out_shape=[
            jax.ShapeDtypeStruct((tok, cols), jnp.bfloat16),
            jax.ShapeDtypeStruct((tok, cols), jnp.bfloat16),
            jax.ShapeDtypeStruct((slots, seg, 2 * cols), jnp.bfloat16),
        ],
        compiler_params=pltpu.CompilerParams(vmem_limit_bytes=VMEM_BYTES),
        name="attention",
    )(ids, target, queries, grad_attn, *([kv] * per_block))


def sum_kernel(count, ids, ret_ref, out_ref, acc):
    acc[...] = jnp.zeros_like(acc)

    @pl.loop(0, count)
    def _(i):
        slot = ids[i]

        @pl.when(slot >= 0)
        def _():
            acc[slot] = acc[slot] + ret_ref[i].astype(jnp.float32)

    out_ref[...] = acc[...].astype(jnp.bfloat16)


def sum_slots(ids, returned, stored):
    shape = (stored,) + returned.shape[1:]
    return pl.pallas_call(
        functools.partial(sum_kernel, returned.shape[0]),
        grid_spec=pltpu.PrefetchScalarGridSpec(
            num_scalar_prefetch=1,
            grid=(1,),
            in_specs=[pl.BlockSpec(returned.shape, lambda i, ids: (0, 0, 0))],
            out_specs=pl.BlockSpec(shape, lambda i, ids: (0, 0, 0)),
            scratch_shapes=[pltpu.VMEM(shape, jnp.float32)],
        ),
        out_shape=jax.ShapeDtypeStruct(shape, jnp.bfloat16),
        compiler_params=pltpu.CompilerParams(vmem_limit_bytes=VMEM_BYTES),
        name="sum_slots",
    )(ids, returned)


def ring_place(n, index):
    return jnp.where(index % 2 == 0, index // 2, n - 1 - index // 2)


def ring_index(n, place):
    return jnp.where(place < n // 2, 2 * place, 2 * (n - 1 - place) + 1)


def ring_setup(n):
    forward = 1 - 2 * (lax.axis_index("dp") % 2)
    place = ring_place(n, lax.axis_index("mp"))
    ahead = ring_index(n, (place + forward + n) % n)
    behind = ring_index(n, (place - forward + n) % n)

    def chunk(step):
        return ring_index(n, (place - forward * (1 + step) + 2 * n) % n)

    return ahead, behind, chunk


def ring_sum(n, ahead, chunk, streams):
    def copy(stream, src, step):
        _, buf, send_sem, recv_sem, _, _ = stream
        return pltpu.make_async_remote_copy(
            src_ref=src,
            dst_ref=buf.at[step],
            send_sem=send_sem.at[step],
            recv_sem=recv_sem.at[step],
            device_id={"mp": ahead},
            device_id_type=pl.DeviceIdType.MESH,
        )

    for stream in streams:
        part, first = stream[0], stream[4]
        first[...] = part(chunk(0)).astype(jnp.bfloat16)
        copy(stream, first, 0).start()

    @pl.loop(1, n - 1)
    def _(step):
        for stream in streams:
            part, buf = stream[:2]
            term = part(chunk(step))
            copy(stream, buf.at[step - 1], step - 1).wait_recv()
            buf[step - 1] = (buf[step - 1].astype(jnp.float32) + term).astype(jnp.bfloat16)
            copy(stream, buf.at[step - 1], step).start()

    for stream in streams:
        part, buf, _, _, first, out = stream
        term = part(chunk(n - 1))
        copy(stream, first, n - 2).wait_recv()
        out[...] = (buf[n - 2].astype(jnp.float32) + term).astype(jnp.bfloat16)

    @pl.loop(0, n - 1)
    def _(step):
        for stream in streams:
            copy(stream, stream[4], step).wait_send()


def exchange_kernel(
    n, owners, attn, gq, w_out, w_query, outgoing, sent_ids,
    att_out, hid_out, returned, returned_ids,
    att_buf, hid_buf, att_first, hid_first, att_send, att_recv, hid_send, hid_recv,
    data_send, data_recv, ids_send, ids_recv, local_sem,
):
    me = lax.axis_index("dp")
    ahead, behind, chunk = ring_setup(n)
    rows = outgoing.shape[0] // owners
    width = att_out.shape[1]

    barrier = pltpu.get_barrier_semaphore()
    for device in [{"mp": ahead}, {"mp": behind}] + [{"dp": (me + d) % owners} for d in range(1, owners)]:
        pl.semaphore_signal(barrier, inc=1, device_id=device, device_id_type=pl.DeviceIdType.MESH)
    pl.semaphore_wait(barrier, 1 + owners)

    def block(index):
        return pl.ds(pl.multiple_of(index * rows, rows), rows)

    copies = []
    for d in range(1, owners):
        to = (me + d) % owners
        for src, dst, send, recv in (
            (outgoing.at[block(to)], returned.at[block(me)], data_send, data_recv),
            (sent_ids.at[to], returned_ids.at[me], ids_send, ids_recv),
        ):
            copies.append(pltpu.make_async_remote_copy(
                src_ref=src,
                dst_ref=dst,
                send_sem=send.at[d - 1],
                recv_sem=recv.at[d - 1],
                device_id={"dp": to},
                device_id_type=pl.DeviceIdType.MESH,
            ))
    local = [
        pltpu.make_async_copy(outgoing.at[block(me)], returned.at[block(me)], local_sem.at[0]),
        pltpu.make_async_copy(sent_ids.at[me], returned_ids.at[me], local_sem.at[1]),
    ]
    for copy in copies + local:
        copy.start()

    def at(index):
        return pl.ds(pl.multiple_of(index * width, width), width)

    ring_sum(n, ahead, chunk, [
        (lambda c: dot(attn[...], w_out[:, at(c)], (1, 0)), att_buf, att_send, att_recv, att_first, att_out),
        (lambda c: dot(gq[...], w_query[at(c), :], (1, 1)), hid_buf, hid_send, hid_recv, hid_first, hid_out),
    ])
    for copy in copies + local:
        copy.wait()


def exchange(attn, gq, w_out, w_query, outgoing, sent_ids):
    n, owners = lax.axis_size("mp"), lax.axis_size("dp")
    tok = attn.shape[0]
    width = w_out.shape[1] // n
    vmem = pl.BlockSpec(memory_space=pltpu.VMEM)
    anywhere = pl.BlockSpec(memory_space=pl.ANY)
    piece = jax.ShapeDtypeStruct((tok, width), jnp.bfloat16)
    ring = pltpu.SemaphoreType.DMA((n - 1,))
    peers = pltpu.SemaphoreType.DMA((owners - 1,))
    return pl.pallas_call(
        functools.partial(exchange_kernel, n, owners),
        in_specs=[vmem] * 4 + [anywhere] * 2,
        out_specs=[vmem, vmem, anywhere, anywhere],
        out_shape=[
            piece,
            piece,
            jax.ShapeDtypeStruct(outgoing.shape, outgoing.dtype),
            jax.ShapeDtypeStruct(sent_ids.shape, sent_ids.dtype),
        ],
        scratch_shapes=[pltpu.VMEM((n - 1, tok, width), jnp.bfloat16)] * 2
        + [pltpu.VMEM((tok, width), jnp.bfloat16)] * 2
        + [ring] * 4
        + [peers] * 4
        + [pltpu.SemaphoreType.DMA((2,))],
        compiler_params=pltpu.CompilerParams(
            collective_id=1, has_side_effects=True, vmem_limit_bytes=VMEM_BYTES
        ),
        name="exchange",
    )(attn, gq, w_out, w_query, outgoing, sent_ids)


def encoded_kernel(n, grads, w_pair, out, buf, first, send_sem, recv_sem):
    ahead, behind, chunk = ring_setup(n)
    barrier = pltpu.get_barrier_semaphore()
    for device in (ahead, behind):
        pl.semaphore_signal(barrier, inc=1, device_id={"mp": device}, device_id_type=pl.DeviceIdType.MESH)
    pl.semaphore_wait(barrier, 2)
    ring_sum(n, ahead, chunk, [
        (lambda c: dot(grads[c], w_pair[...], (1, 1)), buf, send_sem, recv_sem, first, out),
    ])


def encoded_sum(grads, w_pair):
    n = lax.axis_size("mp")
    rows, width = grads.shape[1], w_pair.shape[0]
    vmem = pl.BlockSpec(memory_space=pltpu.VMEM)
    return pl.pallas_call(
        functools.partial(encoded_kernel, n),
        in_specs=[vmem] * 2,
        out_specs=vmem,
        out_shape=jax.ShapeDtypeStruct((rows, width), jnp.bfloat16),
        scratch_shapes=[
            pltpu.VMEM((n - 1, rows, width), jnp.bfloat16),
            pltpu.VMEM((rows, width), jnp.bfloat16),
            pltpu.SemaphoreType.DMA((n - 1,)),
            pltpu.SemaphoreType.DMA((n - 1,)),
        ],
        compiler_params=pltpu.CompilerParams(
            collective_id=2, has_side_effects=True, vmem_limit_bytes=VMEM_BYTES
        ),
        name="encoded_sum",
    )(grads, w_pair)


def shards(hidden, encoded, neighbours, w_query, w_key, w_value, w_out, cotangent):
    owners = lax.axis_size("dp")
    blocks, per_block = neighbours.shape
    requests = blocks * per_block
    capacity = requests // 4
    stored = encoded.shape[0]
    enc_width, head_cols = w_key.shape
    seg_len = encoded.shape[1] // enc_width

    w_pair = jnp.concatenate([w_key, w_value], axis=1)
    enc_rows = encoded.reshape(stored * seg_len, enc_width)
    kv_own = jnp.dot(enc_rows, w_pair, preferred_element_type=jnp.float32).astype(jnp.bfloat16)
    kv = lax.all_gather(kv_own.reshape(stored, seg_len, 2 * head_cols), "dp", axis=0, tiled=True)
    queries = jnp.dot(hidden, w_query, preferred_element_type=jnp.float32).astype(jnp.bfloat16)
    grad_attn = dot(cotangent, w_out, (1, 1)).astype(jnp.bfloat16)

    flat_ids = neighbours.reshape(requests)
    flat_owner = flat_ids // stored
    mine = flat_owner[:, None] == flat_owner[None, :]
    before = jnp.arange(requests)[:, None] > jnp.arange(requests)[None, :]
    target = flat_owner * capacity + jnp.sum((mine & before).astype(jnp.int32), axis=1)
    placed = target[:, None] == jnp.arange(owners * capacity)[None, :]
    sent_ids = jnp.sum(jnp.where(placed, (flat_ids % stored)[:, None] + 1, 0), axis=0) - 1
    sent_ids = jnp.broadcast_to(sent_ids.reshape(owners, 1, capacity), (owners, 8, capacity))
    sent_ids = jnp.pad(sent_ids, ((0, 0), (0, 0), (0, 128 - capacity)))

    attn, grad_query, outgoing = attention(
        flat_ids, target, queries, grad_attn, kv, blocks, owners * capacity
    )
    attended, grad_hidden, returned, returned_ids = exchange(
        attn, grad_query, w_out, w_query, outgoing, sent_ids
    )
    my_slots = returned_ids[:, 0, :capacity].reshape(owners * capacity)
    grad_stored = sum_slots(my_slots, returned, stored)
    parts = lax.axis_size("mp")
    grad_stored = grad_stored.reshape(stored, parts, seg_len // parts, 2 * head_cols)
    grad_stored = grad_stored.transpose(1, 0, 2, 3).reshape(parts, -1, 2 * head_cols)
    grad_encoded = encoded_sum(grad_stored, w_pair)
    return attended, grad_hidden, grad_encoded.reshape(stored, -1)


def solution(mesh):
    placed = (
        P("dp", None),
        P("dp", None),
        P("dp", None),
        P(None, "mp"),
        P(None, "mp"),
        P(None, "mp"),
        P("mp", None),
        P("dp", None),
    )
    return jax.shard_map(
        shards,
        mesh=mesh,
        in_specs=placed,
        out_specs=(P("dp", "mp"), P("dp", "mp"), P("dp", "mp")),
        check_vma=False,
    )
```

```python
import functools
import math

import jax
import jax.numpy as jnp
from jax import lax
from jax.experimental import pallas as pl
from jax.experimental.pallas import tpu as pltpu
from jax.sharding import PartitionSpec as P

DH = 128
VMEM_BYTES = 48 * 1024 * 1024


def dot(a, b, contract):
    return lax.dot_general(a, b, ((contract[:1], contract[1:]), ((), ())), preferred_element_type=jnp.float32)


def attention_kernel(per_block, ids, target, q_ref, ga_ref, *refs):
    kv_refs = refs[:per_block]
    attn_ref, gq_ref, out_ref = refs[per_block:]
    step = pl.program_id(0)
    cols = q_ref.shape[1]
    seg = kv_refs[0].shape[1]
    inv_root = 1.0 / math.sqrt(DH)

    if out_ref.shape[0] > target.shape[0]:
        @pl.when(step == 0)
        def _():
            out_ref[...] = jnp.zeros_like(out_ref)

    for h in range(cols // DH):
        at = h * DH
        q = q_ref[:, at:at + DH]
        ga = ga_ref[:, at:at + DH]
        k = jnp.concatenate([r[0, :, at:at + DH] for r in kv_refs], axis=0)
        v = jnp.concatenate([r[0, :, cols + at:cols + at + DH] for r in kv_refs], axis=0)
        scores = dot(q, k, (1, 1)) * inv_root
        grad_prob = dot(ga, v, (1, 1))
        terms = jnp.exp(scores - jnp.max(scores, axis=-1, keepdims=True))
        prob = terms / jnp.sum(terms, axis=-1, keepdims=True)
        half = prob.astype(jnp.bfloat16)
        attn_ref[:, at:at + DH] = dot(half, v, (1, 0)).astype(jnp.bfloat16)
        grad_v = dot(half, ga, (0, 0)).astype(jnp.bfloat16)
        gs = (prob * (grad_prob - jnp.sum(prob * grad_prob, axis=-1, keepdims=True))).astype(jnp.bfloat16)
        gq_ref[:, at:at + DH] = (dot(gs, k, (1, 0)) * inv_root).astype(jnp.bfloat16)
        grad_k = (dot(gs, q, (0, 0)) * inv_root).astype(jnp.bfloat16)
        for j in range(per_block):
            slot = target[step * per_block + j]
            out_ref[slot, :, at:at + DH] = grad_k[j * seg:(j + 1) * seg]
            out_ref[slot, :, cols + at:cols + at + DH] = grad_v[j * seg:(j + 1) * seg]


def attention(ids, target, queries, grad_attn, kv, blocks, slots):
    per_block = ids.shape[0] // blocks
    tok, cols = queries.shape
    block_len = tok // blocks
    seg = kv.shape[1]
    row = pl.BlockSpec((block_len, cols), lambda c, ids, tg: (c, 0))

    def kv_spec(j):
        return pl.BlockSpec((1, seg, 2 * cols), lambda c, ids, tg: (ids[c * per_block + j], 0, 0))

    return pl.pallas_call(
        functools.partial(attention_kernel, per_block),
        grid_spec=pltpu.PrefetchScalarGridSpec(
            num_scalar_prefetch=2,
            grid=(blocks,),
            in_specs=[row, row] + [kv_spec(j) for j in range(per_block)],
            out_specs=[row, row, pl.BlockSpec((slots, seg, 2 * cols), lambda c, ids, tg: (0, 0, 0))],
        ),
        out_shape=[
            jax.ShapeDtypeStruct((tok, cols), jnp.bfloat16),
            jax.ShapeDtypeStruct((tok, cols), jnp.bfloat16),
            jax.ShapeDtypeStruct((slots, seg, 2 * cols), jnp.bfloat16),
        ],
        compiler_params=pltpu.CompilerParams(vmem_limit_bytes=VMEM_BYTES),
        name="attention",
    )(ids, target, queries, grad_attn, *([kv] * per_block))


def ring_place(n, index):
    return jnp.where(index % 2 == 0, index // 2, n - 1 - index // 2)


def ring_index(n, place):
    return jnp.where(place < n // 2, 2 * place, 2 * (n - 1 - place) + 1)


def ring_setup(n):
    forward = 1 - 2 * (lax.axis_index("dp") % 2)
    place = ring_place(n, lax.axis_index("mp"))
    ahead = ring_index(n, (place + forward + n) % n)
    behind = ring_index(n, (place - forward + n) % n)

    def chunk(step):
        return ring_index(n, (place - forward * (1 + step) + 2 * n) % n)

    return ahead, behind, chunk


class Ring:
    def __init__(self, n, ahead, chunk, part, buf, first, send_sem, recv_sem, out):
        self.n, self.ahead, self.chunk, self.part = n, ahead, chunk, part
        self.buf, self.head, self.send_sem, self.recv_sem, self.out = buf, first, send_sem, recv_sem, out

    def copy(self, src, step):
        return pltpu.make_async_remote_copy(
            src_ref=src,
            dst_ref=self.buf.at[step],
            send_sem=self.send_sem.at[step],
            recv_sem=self.recv_sem.at[step],
            device_id={"mp": self.ahead},
            device_id_type=pl.DeviceIdType.MESH,
        )

    def first(self):
        self.head[...] = self.part(self.chunk(0)).astype(jnp.bfloat16)
        self.copy(self.head, 0).start()

    def middle(self, step):
        term = self.part(self.chunk(step))
        held = self.buf.at[step - 1]
        self.copy(held, step - 1).wait_recv()
        held[...] = (held[...].astype(jnp.float32) + term).astype(jnp.bfloat16)
        self.copy(held, step).start()

    def last(self):
        term = self.part(self.chunk(self.n - 1))
        self.copy(self.head, self.n - 2).wait_recv()
        self.out[...] = (self.buf[self.n - 2].astype(jnp.float32) + term).astype(jnp.bfloat16)

    def drain(self):
        @pl.loop(0, self.n - 1)
        def _(step):
            self.copy(self.head, step).wait_send()


def exchange_kernel(
    n, owners, stored, attn, gq, w_out, w_query, w_pair, outgoing, sent_ids,
    att_out, hid_out, enc_out, returned, returned_ids,
    att_buf, hid_buf, enc_buf, att_first, hid_first, enc_first,
    att_send, att_recv, hid_send, hid_recv, enc_send, enc_recv,
    data_send, data_recv, ids_send, ids_recv, local_sem,
):
    me = lax.axis_index("dp")
    ahead, behind, chunk = ring_setup(n)
    rows = outgoing.shape[0] // owners
    width = att_out.shape[1]

    barrier = pltpu.get_barrier_semaphore()
    for device in [{"mp": ahead}, {"mp": behind}] + [{"dp": (me + d) % owners} for d in range(1, owners)]:
        pl.semaphore_signal(barrier, inc=1, device_id=device, device_id_type=pl.DeviceIdType.MESH)
    pl.semaphore_wait(barrier, 1 + owners)

    def block(index):
        return pl.ds(pl.multiple_of(index * rows, rows), rows)

    copies = []
    for d in range(1, owners):
        to = (me + d) % owners
        for src, dst, send, recv in (
            (outgoing.at[block(to)], returned.at[block(me)], data_send, data_recv),
            (sent_ids.at[to], returned_ids.at[me], ids_send, ids_recv),
        ):
            copies.append(pltpu.make_async_remote_copy(
                src_ref=src,
                dst_ref=dst,
                send_sem=send.at[d - 1],
                recv_sem=recv.at[d - 1],
                device_id={"dp": to},
                device_id_type=pl.DeviceIdType.MESH,
            ))
    local = [
        pltpu.make_async_copy(outgoing.at[block(me)], returned.at[block(me)], local_sem.at[0]),
        pltpu.make_async_copy(sent_ids.at[me], returned_ids.at[me], local_sem.at[1]),
    ]
    for copy in copies + local:
        copy.start()

    def at(index):
        return pl.ds(pl.multiple_of(index * width, width), width)

    tokens = returned.shape[1] // n
    window = max(tokens, 16)
    enc_rows = stored * tokens

    def enc_part(c):
        start = c * tokens
        base = pl.multiple_of(start // 16 * 16, 16)
        shape = (enc_rows, rows * window)
        row = lax.broadcasted_iota(jnp.int32, shape, 0)
        col = lax.broadcasted_iota(jnp.int32, shape, 1)
        same_token = col % window == start - base + row % tokens
        total = None
        for q in range(owners):
            slot = returned_ids[q, 0:1, 0:rows * window]
            hit = jnp.where(same_token & (slot == row // tokens), 1.0, 0.0).astype(jnp.bfloat16)
            block_rows = returned[q * rows:(q + 1) * rows, pl.ds(base, window), :]
            term = dot(hit, block_rows.reshape(rows * window, -1), (1, 0))
            total = term if total is None else total + term
        return dot(total.astype(jnp.bfloat16), w_pair[...], (1, 1))

    att = Ring(n, ahead, chunk, lambda c: dot(attn[...], w_out[:, at(c)], (1, 0)),
               att_buf, att_first, att_send, att_recv, att_out)
    hid = Ring(n, ahead, chunk, lambda c: dot(gq[...], w_query[at(c), :], (1, 1)),
               hid_buf, hid_first, hid_send, hid_recv, hid_out)
    enc = Ring(n, ahead, chunk, enc_part, enc_buf, enc_first, enc_send, enc_recv, enc_out)

    alone = n // 2
    att.first()
    hid.first()

    @pl.loop(1, alone + 1)
    def _(step):
        att.middle(step)
        hid.middle(step)

    for copy in copies + local:
        copy.wait()
    enc.first()

    @pl.loop(alone + 1, n - 1)
    def _(step):
        done = 2 * (step - alone - 1)
        att.middle(step)
        enc.middle(done + 1)
        hid.middle(step)
        enc.middle(done + 2)

    att.last()
    enc.middle(n - 3)
    hid.last()
    enc.middle(n - 2)
    enc.last()
    for ring in (att, hid, enc):
        ring.drain()


def exchange(attn, gq, w_out, w_query, w_pair, outgoing, sent_ids, stored):
    n, owners = lax.axis_size("mp"), lax.axis_size("dp")
    tok = attn.shape[0]
    width = w_out.shape[1] // n
    vmem = pl.BlockSpec(memory_space=pltpu.VMEM)
    anywhere = pl.BlockSpec(memory_space=pl.ANY)
    shapes = [(tok, width), (tok, width), (stored * outgoing.shape[1] // n, w_pair.shape[0])]
    ring = pltpu.SemaphoreType.DMA((n - 1,))
    peers = pltpu.SemaphoreType.DMA((owners - 1,))
    return pl.pallas_call(
        functools.partial(exchange_kernel, n, owners, stored),
        in_specs=[vmem] * 5 + [anywhere] * 2,
        out_specs=[vmem] * 3,
        out_shape=[jax.ShapeDtypeStruct(shape, jnp.bfloat16) for shape in shapes],
        scratch_shapes=[pltpu.VMEM(outgoing.shape, outgoing.dtype), pltpu.VMEM(sent_ids.shape, sent_ids.dtype)]
        + [pltpu.VMEM((n - 1,) + shape, jnp.bfloat16) for shape in shapes]
        + [pltpu.VMEM(shape, jnp.bfloat16) for shape in shapes]
        + [ring] * 6
        + [peers] * 4
        + [pltpu.SemaphoreType.DMA((2,))],
        compiler_params=pltpu.CompilerParams(
            collective_id=1, has_side_effects=True, vmem_limit_bytes=VMEM_BYTES
        ),
        name="exchange",
    )(attn, gq, w_out, w_query, w_pair, outgoing, sent_ids)


def shards(hidden, encoded, neighbours, w_query, w_key, w_value, w_out, cotangent):
    owners = lax.axis_size("dp")
    blocks, per_block = neighbours.shape
    requests = blocks * per_block
    capacity = requests // 4
    stored = encoded.shape[0]
    enc_width, head_cols = w_key.shape
    seg_len = encoded.shape[1] // enc_width

    w_pair = jnp.concatenate([w_key, w_value], axis=1)
    enc_rows = encoded.reshape(stored * seg_len, enc_width)
    kv_own = jnp.dot(enc_rows, w_pair, preferred_element_type=jnp.float32).astype(jnp.bfloat16)
    kv = lax.all_gather(kv_own.reshape(stored, seg_len, 2 * head_cols), "dp", axis=0, tiled=True)
    queries = jnp.dot(hidden, w_query, preferred_element_type=jnp.float32).astype(jnp.bfloat16)
    grad_attn = dot(cotangent, w_out, (1, 1)).astype(jnp.bfloat16)

    flat_ids = neighbours.reshape(requests)
    flat_owner = flat_ids // stored
    mine = flat_owner[:, None] == flat_owner[None, :]
    before = jnp.arange(requests)[:, None] > jnp.arange(requests)[None, :]
    target = flat_owner * capacity + jnp.sum((mine & before).astype(jnp.int32), axis=1)
    placed = target[:, None] == jnp.arange(owners * capacity)[None, :]
    sent_ids = jnp.sum(jnp.where(placed, (flat_ids % stored)[:, None] + 1, 0), axis=0) - 1
    parts = lax.axis_size("mp")
    window = max(seg_len // parts, 16)
    sent_ids = jnp.repeat(sent_ids.reshape(owners, 1, capacity), window, axis=2)
    pad = -capacity * window % 128
    sent_ids = jnp.pad(jnp.broadcast_to(sent_ids, (owners, 8, capacity * window)), ((0, 0), (0, 0), (0, pad)))

    attn, grad_query, outgoing = attention(
        flat_ids, target, queries, grad_attn, kv, blocks, owners * capacity
    )
    attended, grad_hidden, grad_encoded = exchange(
        attn, grad_query, w_out, w_query, w_pair, outgoing, sent_ids, stored
    )
    return attended, grad_hidden, grad_encoded.reshape(stored, -1)


def solution(mesh):
    placed = (
        P("dp", None),
        P("dp", None),
        P("dp", None),
        P(None, "mp"),
        P(None, "mp"),
        P(None, "mp"),
        P("mp", None),
        P("dp", None),
    )
    return jax.shard_map(
        shards,
        mesh=mesh,
        in_specs=placed,
        out_specs=(P("dp", "mp"), P("dp", "mp"), P("dp", "mp")),
        check_vma=False,
    )
```

```python
import functools
import math

import jax
import jax.numpy as jnp
from jax import lax
from jax.experimental import pallas as pl
from jax.experimental.pallas import tpu as pltpu
from jax.sharding import PartitionSpec as P

DH = 128
VMEM_BYTES = 48 * 1024 * 1024


def dot(a, b, contract):
    return lax.dot_general(a, b, ((contract[:1], contract[1:]), ((), ())), preferred_element_type=jnp.float32)


def attention_kernel(per_block, ids, target, q_ref, ga_ref, *refs):
    kv_refs = refs[:per_block]
    attn_ref, gq_ref, out_ref = refs[per_block:]
    step = pl.program_id(0)
    cols = q_ref.shape[1]
    seg = kv_refs[0].shape[1]
    inv_root = 1.0 / math.sqrt(DH)

    if out_ref.shape[0] > target.shape[0]:
        @pl.when(step == 0)
        def _():
            out_ref[...] = jnp.zeros_like(out_ref)

    for h in range(cols // DH):
        at = h * DH
        q = q_ref[:, at:at + DH]
        ga = ga_ref[:, at:at + DH]
        k = jnp.concatenate([r[0, :, at:at + DH] for r in kv_refs], axis=0)
        v = jnp.concatenate([r[0, :, cols + at:cols + at + DH] for r in kv_refs], axis=0)
        scores = dot(q, k, (1, 1)) * inv_root
        grad_prob = dot(ga, v, (1, 1))
        terms = jnp.exp(scores - jnp.max(scores, axis=-1, keepdims=True))
        prob = terms / jnp.sum(terms, axis=-1, keepdims=True)
        half = prob.astype(jnp.bfloat16)
        attn_ref[:, at:at + DH] = dot(half, v, (1, 0)).astype(jnp.bfloat16)
        grad_v = dot(half, ga, (0, 0)).astype(jnp.bfloat16)
        gs = (prob * (grad_prob - jnp.sum(prob * grad_prob, axis=-1, keepdims=True))).astype(jnp.bfloat16)
        gq_ref[:, at:at + DH] = (dot(gs, k, (1, 0)) * inv_root).astype(jnp.bfloat16)
        grad_k = (dot(gs, q, (0, 0)) * inv_root).astype(jnp.bfloat16)
        for j in range(per_block):
            slot = target[step * per_block + j]
            out_ref[slot, :, at:at + DH] = grad_k[j * seg:(j + 1) * seg]
            out_ref[slot, :, cols + at:cols + at + DH] = grad_v[j * seg:(j + 1) * seg]


def attention(ids, target, queries, grad_attn, kv, blocks, slots):
    per_block = ids.shape[0] // blocks
    tok, cols = queries.shape
    block_len = tok // blocks
    seg = kv.shape[1]
    row = pl.BlockSpec((block_len, cols), lambda c, ids, tg: (c, 0))

    def kv_spec(j):
        return pl.BlockSpec((1, seg, 2 * cols), lambda c, ids, tg: (ids[c * per_block + j], 0, 0))

    return pl.pallas_call(
        functools.partial(attention_kernel, per_block),
        grid_spec=pltpu.PrefetchScalarGridSpec(
            num_scalar_prefetch=2,
            grid=(blocks,),
            in_specs=[row, row] + [kv_spec(j) for j in range(per_block)],
            out_specs=[row, row, pl.BlockSpec((slots, seg, 2 * cols), lambda c, ids, tg: (0, 0, 0))],
        ),
        out_shape=[
            jax.ShapeDtypeStruct((tok, cols), jnp.bfloat16),
            jax.ShapeDtypeStruct((tok, cols), jnp.bfloat16),
            jax.ShapeDtypeStruct((slots, seg, 2 * cols), jnp.bfloat16),
        ],
        compiler_params=pltpu.CompilerParams(vmem_limit_bytes=VMEM_BYTES),
        name="attention",
    )(ids, target, queries, grad_attn, *([kv] * per_block))


def ring_place(n, index):
    return jnp.where(index % 2 == 0, index // 2, n - 1 - index // 2)


def ring_index(n, place):
    return jnp.where(place < n // 2, 2 * place, 2 * (n - 1 - place) + 1)


def ring_setup(n):
    forward = 1 - 2 * (lax.axis_index("dp") % 2)
    place = ring_place(n, lax.axis_index("mp"))
    ahead = ring_index(n, (place + forward + n) % n)
    behind = ring_index(n, (place - forward + n) % n)

    def chunk(step):
        return ring_index(n, (place - forward * (1 + step) + 2 * n) % n)

    return ahead, behind, chunk


class Ring:
    def __init__(self, n, ahead, chunk, part, buf, first, send_sem, recv_sem, out):
        self.n, self.ahead, self.chunk, self.part = n, ahead, chunk, part
        self.buf, self.head, self.send_sem, self.recv_sem, self.out = buf, first, send_sem, recv_sem, out

    def copy(self, src, step):
        return pltpu.make_async_remote_copy(
            src_ref=src,
            dst_ref=self.buf.at[step],
            send_sem=self.send_sem.at[step],
            recv_sem=self.recv_sem.at[step],
            device_id={"mp": self.ahead},
            device_id_type=pl.DeviceIdType.MESH,
        )

    def first(self):
        self.head[...] = self.part(self.chunk(0)).astype(jnp.bfloat16)
        self.copy(self.head, 0).start()

    def middle(self, step):
        term = self.part(self.chunk(step))
        held = self.buf.at[step - 1]
        self.copy(held, step - 1).wait_recv()
        held[...] = (held[...].astype(jnp.float32) + term).astype(jnp.bfloat16)
        self.copy(held, step).start()

    def last(self):
        term = self.part(self.chunk(self.n - 1))
        self.copy(self.head, self.n - 2).wait_recv()
        self.out[...] = (self.buf[self.n - 2].astype(jnp.float32) + term).astype(jnp.bfloat16)

    def drain(self):
        @pl.loop(0, self.n - 1)
        def _(step):
            self.copy(self.head, step).wait_send()


def exchange_kernel(
    n, owners, stored, attn, gq, w_out, w_query, w_pair, outgoing, sent_ids,
    att_out, hid_out, enc_out, returned, returned_ids,
    att_buf, hid_buf, enc_buf, att_first, hid_first, enc_first,
    att_send, att_recv, hid_send, hid_recv, enc_send, enc_recv,
    data_send, data_recv, ids_send, ids_recv, local_sem,
):
    me = lax.axis_index("dp")
    ahead, behind, chunk = ring_setup(n)
    rows = outgoing.shape[0] // owners
    width = att_out.shape[1]

    barrier = pltpu.get_barrier_semaphore()
    for device in [{"mp": ahead}, {"mp": behind}] + [{"dp": (me + d) % owners} for d in range(1, owners)]:
        pl.semaphore_signal(barrier, inc=1, device_id=device, device_id_type=pl.DeviceIdType.MESH)
    pl.semaphore_wait(barrier, 1 + owners)

    def block(index):
        return pl.ds(pl.multiple_of(index * rows, rows), rows)

    copies = []
    for d in range(1, owners):
        to = (me + d) % owners
        for src, dst, send, recv in (
            (outgoing.at[block(to)], returned.at[block(me)], data_send, data_recv),
            (sent_ids.at[to], returned_ids.at[me], ids_send, ids_recv),
        ):
            copies.append(pltpu.make_async_remote_copy(
                src_ref=src,
                dst_ref=dst,
                send_sem=send.at[d - 1],
                recv_sem=recv.at[d - 1],
                device_id={"dp": to},
                device_id_type=pl.DeviceIdType.MESH,
            ))
    local = [
        pltpu.make_async_copy(outgoing.at[block(me)], returned.at[block(me)], local_sem.at[0]),
        pltpu.make_async_copy(sent_ids.at[me], returned_ids.at[me], local_sem.at[1]),
    ]
    for copy in copies + local:
        copy.start()

    def at(index):
        return pl.ds(pl.multiple_of(index * width, width), width)

    tokens = returned.shape[1] // n
    window = max(tokens, 16)
    enc_rows = stored * tokens

    def enc_part(c):
        start = c * tokens
        base = pl.multiple_of(start // 16 * 16, 16)
        shape = (enc_rows, rows * window)
        row = lax.broadcasted_iota(jnp.int32, shape, 0)
        col = lax.broadcasted_iota(jnp.int32, shape, 1)
        same_token = col % window == start - base + row % tokens
        total = None
        for q in range(owners):
            slot = returned_ids[q, 0:1, 0:rows * window]
            hit = jnp.where(same_token & (slot == row // tokens), 1.0, 0.0).astype(jnp.bfloat16)
            block_rows = returned[q * rows:(q + 1) * rows, pl.ds(base, window), :]
            term = dot(hit, block_rows.reshape(rows * window, -1), (1, 0))
            total = term if total is None else total + term
        return dot(total.astype(jnp.bfloat16), w_pair[...], (1, 1))

    att = Ring(n, ahead, chunk, lambda c: dot(attn[...], w_out[:, at(c)], (1, 0)),
               att_buf, att_first, att_send, att_recv, att_out)
    hid = Ring(n, ahead, chunk, lambda c: dot(gq[...], w_query[at(c), :], (1, 1)),
               hid_buf, hid_first, hid_send, hid_recv, hid_out)
    enc = Ring(n, ahead, chunk, enc_part, enc_buf, enc_first, enc_send, enc_recv, enc_out)

    alone = n // 2
    att.first()
    hid.first()

    @pl.loop(1, alone + 1)
    def _(step):
        att.middle(step)
        hid.middle(step)

    for copy in copies + local:
        copy.wait()
    enc.first()

    @pl.loop(alone + 1, n - 1)
    def _(step):
        done = 2 * (step - alone - 1)
        att.middle(step)
        enc.middle(done + 1)
        hid.middle(step)
        enc.middle(done + 2)

    att.last()
    enc.middle(n - 3)
    hid.last()
    enc.middle(n - 2)
    enc.last()
    for ring in (att, hid, enc):
        ring.drain()


def exchange(attn, gq, w_out, w_query, w_pair, outgoing, sent_ids, stored):
    n, owners = lax.axis_size("mp"), lax.axis_size("dp")
    tok = attn.shape[0]
    width = w_out.shape[1] // n
    vmem = pl.BlockSpec(memory_space=pltpu.VMEM)
    anywhere = pl.BlockSpec(memory_space=pl.ANY)
    shapes = [(tok, width), (tok, width), (stored * outgoing.shape[1] // n, w_pair.shape[0])]
    ring = pltpu.SemaphoreType.DMA((n - 1,))
    peers = pltpu.SemaphoreType.DMA((owners - 1,))
    return pl.pallas_call(
        functools.partial(exchange_kernel, n, owners, stored),
        in_specs=[vmem] * 5 + [anywhere] * 2,
        out_specs=[vmem] * 3,
        out_shape=[jax.ShapeDtypeStruct(shape, jnp.bfloat16) for shape in shapes],
        scratch_shapes=[pltpu.VMEM(outgoing.shape, outgoing.dtype), pltpu.VMEM(sent_ids.shape, sent_ids.dtype)]
        + [pltpu.VMEM((n - 1,) + shape, jnp.bfloat16) for shape in shapes]
        + [pltpu.VMEM(shape, jnp.bfloat16) for shape in shapes]
        + [ring] * 6
        + [peers] * 4
        + [pltpu.SemaphoreType.DMA((2,))],
        compiler_params=pltpu.CompilerParams(
            collective_id=1, has_side_effects=True, vmem_limit_bytes=VMEM_BYTES
        ),
        name="exchange",
    )(attn, gq, w_out, w_query, w_pair, outgoing, sent_ids)


def fetch_kernel(
    nx, rows, hidden, w_query, cotangent, w_out, w_pair, queries, grad_attn, kv,
    held, hid_v, wq_v, cot_v, wo_v,
    load_sem, x_send, x_recv, y_send, y_recv, own_send, own_recv,
    cx_send, cx_recv, cy_send, cy_recv,
):
    me, mp = lax.axis_index("dp"), lax.axis_index("mp")
    stored, seg, width = rows.shape
    half = stored // 2
    x, core, side = me // 2, me % 2, mp % 2
    twin = {"dp": x * 2 + 1 - core}
    pair = {"mp": mp + 1 - 2 * side}
    away = [{"dp": (x + d) % nx * 2 + core} for d in range(1, nx)]
    source = [(x - d + nx) % nx * 2 for d in range(1, nx)]

    barrier = pltpu.get_barrier_semaphore()
    for device in away + [twin, pair]:
        pl.semaphore_signal(barrier, inc=1, device_id=device, device_id_type=pl.DeviceIdType.MESH)
    pl.semaphore_wait(barrier, nx + 1)

    def send(src, place, sems, index, device):
        return pltpu.make_async_remote_copy(
            src_ref=src,
            dst_ref=held.at[place],
            send_sem=sems[0].at[index],
            recv_sem=sems[1].at[index],
            device_id=device,
            device_id_type=pl.DeviceIdType.MESH,
        )

    def relay(place, sems, index, device):
        return send(held.at[place], place, sems, index, device)

    steps = [(d, r) for r in range(half) for d in range(nx - 1)]
    mine, other = side * half, (1 - side) * half
    x_copies = [
        send(rows.at[mine + r], me * stored + mine + r, (x_send, x_recv), d * half + r, away[d])
        for d, r in steps
    ]
    own = send(rows, pl.ds(me * stored, stored), (own_send, own_recv), 0, twin)
    for copy in x_copies + [own]:
        copy.start()
    loads = [
        pltpu.make_async_copy(src, dst, load_sem.at[i])
        for i, (src, dst) in enumerate(((hidden, hid_v), (w_query, wq_v), (cotangent, cot_v), (w_out, wo_v)))
    ]
    for load in loads:
        load.start()

    def project(src, first, place):
        block = src[pl.ds(first, half)].reshape(half * seg, width)
        out = dot(block, w_pair[...], (1, 0)).astype(jnp.bfloat16)
        kv[pl.ds(place, half)] = out.reshape(half, seg, -1)

    y_copies, cx_copies, cy_copies = [], [], []

    def pass_on(at):
        d, r = steps[at]
        place = (source[d] + core) * stored + mine + r
        x_copies[at].wait_recv()
        y_copies.append(relay(place, (y_send, y_recv), d * half + r, pair))
        cx_copies.append(relay(place, (cx_send, cx_recv), d * half + r, twin))
        y_copies[-1].start()
        cx_copies[-1].start()

    def finish(at):
        d, r = steps[at]
        place = (source[d] + core) * stored + other + r
        y_copies[at].wait_recv()
        cy_copies.append(relay(place, (cy_send, cy_recv), d * half + r, twin))
        cy_copies[-1].start()

    @pl.loop(0, 2)
    def _(i):
        project(rows, i * half, me * stored + i * half)

    quarter = len(steps) // 4
    pass_next = 0
    for _ in range(quarter):
        pass_on(pass_next)
        pass_next += 1
    loads[0].wait()
    loads[1].wait()
    queries[...] = dot(hid_v[...], wq_v[...], (1, 0)).astype(jnp.bfloat16)
    for _ in range(quarter):
        pass_on(pass_next)
        pass_next += 1
    loads[2].wait()
    loads[3].wait()
    grad_attn[...] = dot(cot_v[...], wo_v[...], (1, 1)).astype(jnp.bfloat16)
    for _ in range(quarter):
        pass_on(pass_next)
        pass_next += 1
    own.wait_recv()

    @pl.loop(0, 2)
    def _(i):
        first = (x * 2 + 1 - core) * stored + i * half
        project(held, first, first)

    while pass_next < len(steps):
        pass_on(pass_next)
        pass_next += 1
    early = max(len(steps) - nx + 1, 0)
    for at in range(early):
        finish(at)
    for copy in cx_copies:
        copy.wait_recv()

    def project_all(first):
        for d in range(nx - 1):
            @pl.loop(0, 2)
            def _(i):
                place = (source[d] + i) * stored + first
                project(held, place, place)

    project_all(mine)
    for at in range(early, len(steps)):
        finish(at)
    for copy in cy_copies:
        copy.wait_recv()
    project_all(other)
    for copy in x_copies + [own] + y_copies + cx_copies + cy_copies:
        copy.wait_send()


def fetch(rows, hidden, w_query, cotangent, w_out, w_pair):
    owners = lax.axis_size("dp")
    nx = owners // 2
    stored, seg, _ = rows.shape
    vmem = pl.BlockSpec(memory_space=pltpu.VMEM)
    anywhere = pl.BlockSpec(memory_space=pl.ANY)
    tok, cols = hidden.shape[0], w_query.shape[1]
    pieces = pltpu.SemaphoreType.DMA(((nx - 1) * stored // 2,))
    return pl.pallas_call(
        functools.partial(fetch_kernel, nx),
        in_specs=[vmem] + [anywhere] * 4 + [vmem],
        out_specs=[vmem] * 3,
        out_shape=[
            jax.ShapeDtypeStruct((tok, cols), jnp.bfloat16),
            jax.ShapeDtypeStruct((tok, cols), jnp.bfloat16),
            jax.ShapeDtypeStruct((owners * stored, seg, w_pair.shape[1]), jnp.bfloat16),
        ],
        scratch_shapes=[pltpu.VMEM((owners * stored,) + rows.shape[1:], jnp.bfloat16)]
        + [pltpu.VMEM(a.shape, a.dtype) for a in (hidden, w_query, cotangent, w_out)]
        + [pltpu.SemaphoreType.DMA((4,))]
        + [pieces] * 4
        + [pltpu.SemaphoreType.DMA((1,))] * 2
        + [pieces] * 4,
        compiler_params=pltpu.CompilerParams(
            collective_id=3, has_side_effects=True, vmem_limit_bytes=VMEM_BYTES
        ),
        name="fetch",
    )(rows, hidden, w_query, cotangent, w_out, w_pair)


def shards(hidden, encoded, neighbours, w_query, w_key, w_value, w_out, cotangent):
    owners = lax.axis_size("dp")
    blocks, per_block = neighbours.shape
    requests = blocks * per_block
    capacity = requests // 4
    stored = encoded.shape[0]
    enc_width, head_cols = w_key.shape
    seg_len = encoded.shape[1] // enc_width

    w_pair = jnp.concatenate([w_key, w_value], axis=1)
    queries, grad_attn, kv = fetch(
        encoded.reshape(stored, seg_len, enc_width), hidden, w_query, cotangent, w_out, w_pair
    )
    flat_ids = neighbours.reshape(requests)
    flat_owner = flat_ids // stored
    mine = flat_owner[:, None] == flat_owner[None, :]
    before = jnp.arange(requests)[:, None] > jnp.arange(requests)[None, :]
    target = flat_owner * capacity + jnp.sum((mine & before).astype(jnp.int32), axis=1)
    placed = target[:, None] == jnp.arange(owners * capacity)[None, :]
    sent_ids = jnp.sum(jnp.where(placed, (flat_ids % stored)[:, None] + 1, 0), axis=0) - 1
    parts = lax.axis_size("mp")
    window = max(seg_len // parts, 16)
    sent_ids = jnp.repeat(sent_ids.reshape(owners, 1, capacity), window, axis=2)
    pad = -capacity * window % 128
    sent_ids = jnp.pad(jnp.broadcast_to(sent_ids, (owners, 8, capacity * window)), ((0, 0), (0, 0), (0, pad)))

    attn, grad_query, outgoing = attention(
        flat_ids, target, queries, grad_attn, kv, blocks, owners * capacity
    )
    attended, grad_hidden, grad_encoded = exchange(
        attn, grad_query, w_out, w_query, w_pair, outgoing, sent_ids, stored
    )
    return attended, grad_hidden, grad_encoded.reshape(stored, -1)


def solution(mesh):
    placed = (
        P("dp", None),
        P("dp", None),
        P("dp", None),
        P(None, "mp"),
        P(None, "mp"),
        P(None, "mp"),
        P("mp", None),
        P("dp", None),
    )
    return jax.shard_map(
        shards,
        mesh=mesh,
        in_specs=placed,
        out_specs=(P("dp", "mp"), P("dp", "mp"), P("dp", "mp")),
        check_vma=False,
    )
```

```python
import functools
import math

import jax
import jax.numpy as jnp
from jax import lax
from jax.experimental import pallas as pl
from jax.experimental.pallas import tpu as pltpu
from jax.sharding import PartitionSpec as P

DH = 128
VMEM_BYTES = 48 * 1024 * 1024


def dot(a, b, contract):
    return lax.dot_general(a, b, ((contract[:1], contract[1:]), ((), ())), preferred_element_type=jnp.float32)


def attention_kernel(per_block, ids, target, q_ref, ga_ref, *refs):
    kv_refs = refs[:per_block]
    attn_ref, gq_ref, out_ref = refs[per_block:]
    step = pl.program_id(0)
    cols = q_ref.shape[1]
    seg = kv_refs[0].shape[1]
    inv_root = 1.0 / math.sqrt(DH)

    if out_ref.shape[0] > target.shape[0]:
        @pl.when(step == 0)
        def _():
            out_ref[...] = jnp.zeros_like(out_ref)

    heads = range(0, cols, DH)
    q = [q_ref[:, at:at + DH] for at in heads]
    ga = [ga_ref[:, at:at + DH] for at in heads]
    k = [jnp.concatenate([r[0, :, at:at + DH] for r in kv_refs], axis=0) for at in heads]
    v = [jnp.concatenate([r[0, :, cols + at:cols + at + DH] for r in kv_refs], axis=0) for at in heads]
    scores = [dot(a, b, (1, 1)) * inv_root for a, b in zip(q, k)]
    grad_prob = [dot(a, b, (1, 1)) for a, b in zip(ga, v)]
    terms = [jnp.exp(a - jnp.max(a, axis=-1, keepdims=True)) for a in scores]
    prob = [a / jnp.sum(a, axis=-1, keepdims=True) for a in terms]
    half = [a.astype(jnp.bfloat16) for a in prob]
    inner = [jnp.sum(a * b, axis=-1, keepdims=True) for a, b in zip(prob, grad_prob)]
    gs = [(a * (b - c)).astype(jnp.bfloat16) for a, b, c in zip(prob, grad_prob, inner)]
    for h, at in enumerate(heads):
        attn_ref[:, at:at + DH] = dot(half[h], v[h], (1, 0)).astype(jnp.bfloat16)
        gq_ref[:, at:at + DH] = (dot(gs[h], k[h], (1, 0)) * inv_root).astype(jnp.bfloat16)
    for h, at in enumerate(heads):
        grad_v = dot(half[h], ga[h], (0, 0)).astype(jnp.bfloat16)
        grad_k = (dot(gs[h], q[h], (0, 0)) * inv_root).astype(jnp.bfloat16)
        for j in range(per_block):
            slot = target[step * per_block + j]
            out_ref[slot, :, at:at + DH] = grad_k[j * seg:(j + 1) * seg]
            out_ref[slot, :, cols + at:cols + at + DH] = grad_v[j * seg:(j + 1) * seg]


def attention(ids, target, queries, grad_attn, kv, blocks, slots):
    per_block = ids.shape[0] // blocks
    tok, cols = queries.shape
    block_len = tok // blocks
    seg = kv.shape[1]
    row = pl.BlockSpec((block_len, cols), lambda c, ids, tg: (c, 0))

    def kv_spec(j):
        return pl.BlockSpec((1, seg, 2 * cols), lambda c, ids, tg: (ids[c * per_block + j], 0, 0))

    return pl.pallas_call(
        functools.partial(attention_kernel, per_block),
        grid_spec=pltpu.PrefetchScalarGridSpec(
            num_scalar_prefetch=2,
            grid=(blocks,),
            in_specs=[row, row] + [kv_spec(j) for j in range(per_block)],
            out_specs=[row, row, pl.BlockSpec((slots, seg, 2 * cols), lambda c, ids, tg: (0, 0, 0))],
        ),
        out_shape=[
            jax.ShapeDtypeStruct((tok, cols), jnp.bfloat16),
            jax.ShapeDtypeStruct((tok, cols), jnp.bfloat16),
            jax.ShapeDtypeStruct((slots, seg, 2 * cols), jnp.bfloat16),
        ],
        compiler_params=pltpu.CompilerParams(vmem_limit_bytes=VMEM_BYTES),
        name="attention",
    )(ids, target, queries, grad_attn, *([kv] * per_block))


def ring_place(n, index):
    return jnp.where(index % 2 == 0, index // 2, n - 1 - index // 2)


def ring_index(n, place):
    return jnp.where(place < n // 2, 2 * place, 2 * (n - 1 - place) + 1)


def ring_setup(n):
    forward = 1 - 2 * (lax.axis_index("dp") % 2)
    place = ring_place(n, lax.axis_index("mp"))
    ahead = ring_index(n, (place + forward + n) % n)
    behind = ring_index(n, (place - forward + n) % n)

    def chunk(step):
        return ring_index(n, (place - forward * (1 + step) + 2 * n) % n)

    return ahead, behind, chunk


class Ring:
    def __init__(self, n, ahead, chunk, part, buf, first, send_sem, recv_sem, out):
        self.n, self.ahead, self.chunk, self.part = n, ahead, chunk, part
        self.buf, self.head, self.send_sem, self.recv_sem, self.out = buf, first, send_sem, recv_sem, out

    def copy(self, src, step):
        return pltpu.make_async_remote_copy(
            src_ref=src,
            dst_ref=self.buf.at[step],
            send_sem=self.send_sem.at[step],
            recv_sem=self.recv_sem.at[step],
            device_id={"mp": self.ahead},
            device_id_type=pl.DeviceIdType.MESH,
        )

    def first(self):
        self.head[...] = self.part(self.chunk(0)).astype(jnp.bfloat16)
        self.copy(self.head, 0).start()

    def middle(self, step):
        term = self.part(self.chunk(step))
        held = self.buf.at[step - 1]
        self.copy(held, step - 1).wait_recv()
        held[...] = (held[...].astype(jnp.float32) + term).astype(jnp.bfloat16)
        self.copy(held, step).start()

    def last(self):
        term = self.part(self.chunk(self.n - 1))
        self.copy(self.head, self.n - 2).wait_recv()
        self.out[...] = (self.buf[self.n - 2].astype(jnp.float32) + term).astype(jnp.bfloat16)

    def drain(self):
        @pl.loop(0, self.n - 1)
        def _(step):
            self.copy(self.head, step).wait_send()


def exchange_kernel(
    n, owners, stored, attn, gq, w_out_hbm, w_query_hbm, w_pair, outgoing, sent_ids,
    att_out, hid_out, enc_out, w_out, w_query, load_sem, returned, returned_ids,
    att_buf, hid_buf, enc_buf, att_first, hid_first, enc_first,
    att_send, att_recv, hid_send, hid_recv, enc_send, enc_recv,
    data_send, data_recv, ids_send, ids_recv, local_sem,
):
    me = lax.axis_index("dp")
    ahead, behind, chunk = ring_setup(n)
    rows = outgoing.shape[0] // owners
    width = att_out.shape[1]

    barrier = pltpu.get_barrier_semaphore()
    for device in [{"mp": ahead}, {"mp": behind}] + [{"dp": (me + d) % owners} for d in range(1, owners)]:
        pl.semaphore_signal(barrier, inc=1, device_id=device, device_id_type=pl.DeviceIdType.MESH)
    pl.semaphore_wait(barrier, 1 + owners)
    loads = [
        pltpu.make_async_copy(w_out_hbm, w_out, load_sem.at[0]),
        pltpu.make_async_copy(w_query_hbm, w_query, load_sem.at[1]),
    ]
    for load in loads:
        load.start()

    def block(index):
        return pl.ds(pl.multiple_of(index * rows, rows), rows)

    copies = []
    for d in range(1, owners):
        to = (me + d) % owners
        for src, dst, send, recv in (
            (outgoing.at[block(to)], returned.at[block(me)], data_send, data_recv),
            (sent_ids.at[to], returned_ids.at[me], ids_send, ids_recv),
        ):
            copies.append(pltpu.make_async_remote_copy(
                src_ref=src,
                dst_ref=dst,
                send_sem=send.at[d - 1],
                recv_sem=recv.at[d - 1],
                device_id={"dp": to},
                device_id_type=pl.DeviceIdType.MESH,
            ))
    local = [
        pltpu.make_async_copy(outgoing.at[block(me)], returned.at[block(me)], local_sem.at[0]),
        pltpu.make_async_copy(sent_ids.at[me], returned_ids.at[me], local_sem.at[1]),
    ]
    for copy in copies + local:
        copy.start()

    def at(index):
        return pl.ds(pl.multiple_of(index * width, width), width)

    tokens = returned.shape[1] // n
    window = max(tokens, 16)
    enc_rows = stored * tokens

    def enc_part(c):
        start = c * tokens
        base = pl.multiple_of(start // 16 * 16, 16)
        shape = (enc_rows, rows * window)
        row = lax.broadcasted_iota(jnp.int32, shape, 0)
        col = lax.broadcasted_iota(jnp.int32, shape, 1)
        same_token = col % window == start - base + row % tokens
        total = None
        for q in range(owners):
            slot = returned_ids[q, 0:1, 0:rows * window]
            hit = jnp.where(same_token & (slot == row // tokens), 1.0, 0.0).astype(jnp.bfloat16)
            block_rows = returned[q * rows:(q + 1) * rows, pl.ds(base, window), :]
            term = dot(hit, block_rows.reshape(rows * window, -1), (1, 0))
            total = term if total is None else total + term
        return dot(total.astype(jnp.bfloat16), w_pair[...], (1, 1))

    att = Ring(n, ahead, chunk, lambda c: dot(attn[...], w_out[:, at(c)], (1, 0)),
               att_buf, att_first, att_send, att_recv, att_out)
    hid = Ring(n, ahead, chunk, lambda c: dot(gq[...], w_query[at(c), :], (1, 1)),
               hid_buf, hid_first, hid_send, hid_recv, hid_out)
    enc = Ring(n, ahead, chunk, enc_part, enc_buf, enc_first, enc_send, enc_recv, enc_out)

    alone = n // 2 - 1
    loads[0].wait()
    att.first()
    loads[1].wait()
    hid.first()

    @pl.loop(1, alone + 1)
    def _(step):
        att.middle(step)
        hid.middle(step)

    att.middle(alone + 1)
    for copy in copies + local:
        copy.wait()
    enc.first()
    hid.middle(alone + 1)
    enc.middle(1)

    @pl.loop(alone + 2, n - 1)
    def _(step):
        done = 2 * (step - alone - 1)
        att.middle(step)
        enc.middle(done)
        hid.middle(step)
        enc.middle(done + 1)

    att.last()
    enc.middle(n - 2)
    hid.last()
    enc.last()
    for ring in (att, hid, enc):
        ring.drain()


def exchange(attn, gq, w_out, w_query, w_pair, outgoing, sent_ids, stored):
    n, owners = lax.axis_size("mp"), lax.axis_size("dp")
    tok = attn.shape[0]
    width = w_out.shape[1] // n
    vmem = pl.BlockSpec(memory_space=pltpu.VMEM)
    anywhere = pl.BlockSpec(memory_space=pl.ANY)
    shapes = [(tok, width), (tok, width), (stored * outgoing.shape[1] // n, w_pair.shape[0])]
    ring = pltpu.SemaphoreType.DMA((n - 1,))
    peers = pltpu.SemaphoreType.DMA((owners - 1,))
    return pl.pallas_call(
        functools.partial(exchange_kernel, n, owners, stored),
        in_specs=[vmem] * 2 + [anywhere] * 2 + [vmem] + [anywhere] * 2,
        out_specs=[vmem] * 3,
        out_shape=[jax.ShapeDtypeStruct(shape, jnp.bfloat16) for shape in shapes],
        scratch_shapes=[pltpu.VMEM(w.shape, w.dtype) for w in (w_out, w_query)]
        + [pltpu.SemaphoreType.DMA((2,))]
        + [pltpu.VMEM(outgoing.shape, outgoing.dtype), pltpu.VMEM(sent_ids.shape, sent_ids.dtype)]
        + [pltpu.VMEM((n - 1,) + shape, jnp.bfloat16) for shape in shapes]
        + [pltpu.VMEM(shape, jnp.bfloat16) for shape in shapes]
        + [ring] * 6
        + [peers] * 4
        + [pltpu.SemaphoreType.DMA((2,))],
        compiler_params=pltpu.CompilerParams(
            collective_id=1, has_side_effects=True, vmem_limit_bytes=VMEM_BYTES
        ),
        name="exchange",
    )(attn, gq, w_out, w_query, w_pair, outgoing, sent_ids)


def fetch_kernel(
    nx, rows, hidden, w_query, cotangent, w_out, w_pair, queries, grad_attn, kv,
    held, hid_v, wq_v, cot_v, wo_v,
    load_sem, x_send, x_recv, y_send, y_recv, own_send, own_recv,
    cx_send, cx_recv, cy_send, cy_recv,
):
    me, mp = lax.axis_index("dp"), lax.axis_index("mp")
    stored, seg, width = rows.shape
    half = stored // 2
    x, core, side = me // 2, me % 2, mp % 2
    twin = {"dp": x * 2 + 1 - core}
    pair = {"mp": mp + 1 - 2 * side}
    away = [{"dp": (x + d) % nx * 2 + core} for d in range(1, nx)]
    source = [(x - d + nx) % nx * 2 for d in range(1, nx)]

    barrier = pltpu.get_barrier_semaphore()
    for device in away + [twin, pair]:
        pl.semaphore_signal(barrier, inc=1, device_id=device, device_id_type=pl.DeviceIdType.MESH)
    pl.semaphore_wait(barrier, nx + 1)

    def send(src, place, sems, index, device):
        return pltpu.make_async_remote_copy(
            src_ref=src,
            dst_ref=held.at[place],
            send_sem=sems[0].at[index],
            recv_sem=sems[1].at[index],
            device_id=device,
            device_id_type=pl.DeviceIdType.MESH,
        )

    def relay(place, sems, index, device):
        return send(held.at[place], place, sems, index, device)

    steps = [(d, r) for r in range(half) for d in range(nx - 1)]
    mine, other = side * half, (1 - side) * half
    x_copies = [
        send(rows.at[mine + r], me * stored + mine + r, (x_send, x_recv), d * half + r, away[d])
        for d, r in steps
    ]
    own = send(rows, pl.ds(me * stored, stored), (own_send, own_recv), 0, twin)
    for copy in x_copies + [own]:
        copy.start()
    loads = [
        pltpu.make_async_copy(src, dst, load_sem.at[i])
        for i, (src, dst) in enumerate(((hidden, hid_v), (w_query, wq_v), (cotangent, cot_v), (w_out, wo_v)))
    ]
    for load in loads:
        load.start()

    def project(src, first, place):
        block = src[pl.ds(first, half)].reshape(half * seg, width)
        out = dot(block, w_pair[...], (1, 0)).astype(jnp.bfloat16)
        kv[pl.ds(place, half)] = out.reshape(half, seg, -1)

    y_copies, cx_copies, cy_copies = [], [], []

    def pass_on(at):
        d, r = steps[at]
        place = (source[d] + core) * stored + mine + r
        x_copies[at].wait_recv()
        y_copies.append(relay(place, (y_send, y_recv), d * half + r, pair))
        cx_copies.append(relay(place, (cx_send, cx_recv), d * half + r, twin))
        y_copies[-1].start()
        cx_copies[-1].start()

    def finish(at):
        d, r = steps[at]
        place = (source[d] + core) * stored + other + r
        y_copies[at].wait_recv()
        cy_copies.append(relay(place, (cy_send, cy_recv), d * half + r, twin))
        cy_copies[-1].start()

    @pl.loop(0, 2)
    def _(i):
        project(rows, i * half, me * stored + i * half)

    quarter = len(steps) // 4
    pass_next = 0
    for _ in range(quarter):
        pass_on(pass_next)
        pass_next += 1
    loads[0].wait()
    loads[1].wait()
    queries[...] = dot(hid_v[...], wq_v[...], (1, 0)).astype(jnp.bfloat16)
    for _ in range(quarter):
        pass_on(pass_next)
        pass_next += 1
    loads[2].wait()
    loads[3].wait()
    grad_attn[...] = dot(cot_v[...], wo_v[...], (1, 1)).astype(jnp.bfloat16)
    for _ in range(quarter):
        pass_on(pass_next)
        pass_next += 1
    own.wait_recv()

    @pl.loop(0, 2)
    def _(i):
        first = (x * 2 + 1 - core) * stored + i * half
        project(held, first, first)

    while pass_next < len(steps):
        pass_on(pass_next)
        pass_next += 1
    early = max(len(steps) - nx + 1, 0)
    for at in range(early):
        finish(at)
    for copy in cx_copies:
        copy.wait_recv()

    def project_all(first):
        for d in range(nx - 1):
            @pl.loop(0, 2)
            def _(i):
                place = (source[d] + i) * stored + first
                project(held, place, place)

    project_all(mine)
    for at in range(early, len(steps)):
        finish(at)
    for copy in cy_copies:
        copy.wait_recv()
    project_all(other)
    for copy in x_copies + [own] + y_copies + cx_copies + cy_copies:
        copy.wait_send()


def fetch(rows, hidden, w_query, cotangent, w_out, w_pair):
    owners = lax.axis_size("dp")
    nx = owners // 2
    stored, seg, _ = rows.shape
    vmem = pl.BlockSpec(memory_space=pltpu.VMEM)
    anywhere = pl.BlockSpec(memory_space=pl.ANY)
    tok, cols = hidden.shape[0], w_query.shape[1]
    pieces = pltpu.SemaphoreType.DMA(((nx - 1) * stored // 2,))
    return pl.pallas_call(
        functools.partial(fetch_kernel, nx),
        in_specs=[vmem] + [anywhere] * 4 + [vmem],
        out_specs=[vmem] * 3,
        out_shape=[
            jax.ShapeDtypeStruct((tok, cols), jnp.bfloat16),
            jax.ShapeDtypeStruct((tok, cols), jnp.bfloat16),
            jax.ShapeDtypeStruct((owners * stored, seg, w_pair.shape[1]), jnp.bfloat16),
        ],
        scratch_shapes=[pltpu.VMEM((owners * stored,) + rows.shape[1:], jnp.bfloat16)]
        + [pltpu.VMEM(a.shape, a.dtype) for a in (hidden, w_query, cotangent, w_out)]
        + [pltpu.SemaphoreType.DMA((4,))]
        + [pieces] * 4
        + [pltpu.SemaphoreType.DMA((1,))] * 2
        + [pieces] * 4,
        compiler_params=pltpu.CompilerParams(
            collective_id=3, has_side_effects=True, vmem_limit_bytes=VMEM_BYTES
        ),
        name="fetch",
    )(rows, hidden, w_query, cotangent, w_out, w_pair)


def shards(hidden, encoded, neighbours, w_query, w_key, w_value, w_out, cotangent):
    owners = lax.axis_size("dp")
    blocks, per_block = neighbours.shape
    requests = blocks * per_block
    capacity = requests // 4
    stored = encoded.shape[0]
    enc_width, head_cols = w_key.shape
    seg_len = encoded.shape[1] // enc_width

    w_pair = jnp.concatenate([w_key, w_value], axis=1)
    queries, grad_attn, kv = fetch(
        encoded.reshape(stored, seg_len, enc_width), hidden, w_query, cotangent, w_out, w_pair
    )
    flat_ids = neighbours.reshape(requests)
    flat_owner = flat_ids // stored
    mine = flat_owner[:, None] == flat_owner[None, :]
    before = jnp.arange(requests)[:, None] > jnp.arange(requests)[None, :]
    target = flat_owner * capacity + jnp.sum((mine & before).astype(jnp.int32), axis=1)
    placed = target[:, None] == jnp.arange(owners * capacity)[None, :]
    sent_ids = jnp.sum(jnp.where(placed, (flat_ids % stored)[:, None] + 1, 0), axis=0) - 1
    parts = lax.axis_size("mp")
    window = max(seg_len // parts, 16)
    sent_ids = jnp.repeat(sent_ids.reshape(owners, 1, capacity), window, axis=2)
    pad = -capacity * window % 128
    sent_ids = jnp.pad(jnp.broadcast_to(sent_ids, (owners, 8, capacity * window)), ((0, 0), (0, 0), (0, pad)))

    attn, grad_query, outgoing = attention(
        flat_ids, target, queries, grad_attn, kv, blocks, owners * capacity
    )
    attended, grad_hidden, grad_encoded = exchange(
        attn, grad_query, w_out, w_query, w_pair, outgoing, sent_ids, stored
    )
    return attended, grad_hidden, grad_encoded.reshape(stored, -1)


def solution(mesh):
    placed = (
        P("dp", None),
        P("dp", None),
        P("dp", None),
        P(None, "mp"),
        P(None, "mp"),
        P(None, "mp"),
        P("mp", None),
        P("dp", None),
    )
    return jax.shard_map(
        shards,
        mesh=mesh,
        in_specs=placed,
        out_specs=(P("dp", "mp"), P("dp", "mp"), P("dp", "mp")),
        check_vma=False,
    )
```

```python
import functools
import math

import jax
import jax.numpy as jnp
from jax import lax
from jax.experimental import pallas as pl
from jax.experimental.pallas import tpu as pltpu
from jax.sharding import PartitionSpec as P

DH = 128
VMEM_BYTES = 48 * 1024 * 1024


def dot(a, b, contract):
    return lax.dot_general(a, b, ((contract[:1], contract[1:]), ((), ())), preferred_element_type=jnp.float32)


def attention_kernel(per_block, ids, target, q_ref, ga_ref, *refs):
    kv_refs = refs[:per_block]
    attn_ref, gq_ref, out_ref = refs[per_block:]
    step = pl.program_id(0)
    cols = q_ref.shape[1]
    seg = kv_refs[0].shape[1]
    inv_root = 1.0 / math.sqrt(DH)

    if out_ref.shape[0] > target.shape[0]:
        @pl.when(step == 0)
        def _():
            out_ref[...] = jnp.zeros_like(out_ref)

    heads = range(0, cols, DH)
    q = [q_ref[:, at:at + DH] for at in heads]
    ga = [ga_ref[:, at:at + DH] for at in heads]
    k = [jnp.concatenate([r[0, :, at:at + DH] for r in kv_refs], axis=0) for at in heads]
    v = [jnp.concatenate([r[0, :, cols + at:cols + at + DH] for r in kv_refs], axis=0) for at in heads]
    scores = [dot(a, b, (1, 1)) * inv_root for a, b in zip(q, k)]
    grad_prob = [dot(a, b, (1, 1)) for a, b in zip(ga, v)]
    terms = [jnp.exp(a - jnp.max(a, axis=-1, keepdims=True)) for a in scores]
    prob = [a / jnp.sum(a, axis=-1, keepdims=True) for a in terms]
    half = [a.astype(jnp.bfloat16) for a in prob]
    inner = [jnp.sum(a * b, axis=-1, keepdims=True) for a, b in zip(prob, grad_prob)]
    gs = [(a * (b - c)).astype(jnp.bfloat16) for a, b, c in zip(prob, grad_prob, inner)]
    for h, at in enumerate(heads):
        attn_ref[:, at:at + DH] = dot(half[h], v[h], (1, 0)).astype(jnp.bfloat16)
        gq_ref[:, at:at + DH] = (dot(gs[h], k[h], (1, 0)) * inv_root).astype(jnp.bfloat16)
    for h, at in enumerate(heads):
        grad_v = dot(half[h], ga[h], (0, 0)).astype(jnp.bfloat16)
        grad_k = (dot(gs[h], q[h], (0, 0)) * inv_root).astype(jnp.bfloat16)
        for j in range(per_block):
            slot = target[step * per_block + j]
            out_ref[slot, :, at:at + DH] = grad_k[j * seg:(j + 1) * seg]
            out_ref[slot, :, cols + at:cols + at + DH] = grad_v[j * seg:(j + 1) * seg]


def attention(ids, target, queries, grad_attn, kv, blocks, slots):
    per_block = ids.shape[0] // blocks
    tok, cols = queries.shape
    block_len = tok // blocks
    seg = kv.shape[1]
    row = pl.BlockSpec((block_len, cols), lambda c, ids, tg: (c, 0))

    def kv_spec(j):
        return pl.BlockSpec((1, seg, 2 * cols), lambda c, ids, tg: (ids[c * per_block + j], 0, 0))

    return pl.pallas_call(
        functools.partial(attention_kernel, per_block),
        grid_spec=pltpu.PrefetchScalarGridSpec(
            num_scalar_prefetch=2,
            grid=(blocks,),
            in_specs=[row, row] + [kv_spec(j) for j in range(per_block)],
            out_specs=[row, row, pl.BlockSpec((slots, seg, 2 * cols), lambda c, ids, tg: (0, 0, 0))],
        ),
        out_shape=[
            jax.ShapeDtypeStruct((tok, cols), jnp.bfloat16),
            jax.ShapeDtypeStruct((tok, cols), jnp.bfloat16),
            jax.ShapeDtypeStruct((slots, seg, 2 * cols), jnp.bfloat16),
        ],
        compiler_params=pltpu.CompilerParams(vmem_limit_bytes=VMEM_BYTES),
        name="attention",
    )(ids, target, queries, grad_attn, *([kv] * per_block))


def ring_place(n, index):
    return jnp.where(index % 2 == 0, index // 2, n - 1 - index // 2)


def ring_index(n, place):
    return jnp.where(place < n // 2, 2 * place, 2 * (n - 1 - place) + 1)


def ring_setup(n):
    forward = 1 - 2 * (lax.axis_index("dp") % 2)
    place = ring_place(n, lax.axis_index("mp"))
    ahead = ring_index(n, (place + forward + n) % n)
    behind = ring_index(n, (place - forward + n) % n)

    def chunk(step):
        return ring_index(n, (place - forward * (1 + step) + 2 * n) % n)

    return ahead, behind, chunk


class Ring:
    def __init__(self, n, ahead, chunk, part, buf, first, send_sem, recv_sem, out):
        self.n, self.ahead, self.chunk, self.part = n, ahead, chunk, part
        self.buf, self.head, self.send_sem, self.recv_sem, self.out = buf, first, send_sem, recv_sem, out

    def copy(self, src, step):
        return pltpu.make_async_remote_copy(
            src_ref=src,
            dst_ref=self.buf.at[step],
            send_sem=self.send_sem.at[step],
            recv_sem=self.recv_sem.at[step],
            device_id={"mp": self.ahead},
            device_id_type=pl.DeviceIdType.MESH,
        )

    def first(self):
        self.head[...] = self.part(self.chunk(0)).astype(jnp.bfloat16)
        self.copy(self.head, 0).start()

    def middle(self, step):
        term = self.part(self.chunk(step))
        held = self.buf.at[step - 1]
        self.copy(held, step - 1).wait_recv()
        held[...] = (held[...].astype(jnp.float32) + term).astype(jnp.bfloat16)
        self.copy(held, step).start()

    def last(self):
        term = self.part(self.chunk(self.n - 1))
        self.copy(self.head, self.n - 2).wait_recv()
        self.out[...] = (self.buf[self.n - 2].astype(jnp.float32) + term).astype(jnp.bfloat16)

    def drain(self):
        @pl.loop(0, self.n - 1)
        def _(step):
            self.copy(self.head, step).wait_send()


def exchange_kernel(
    n, owners, stored, attn, gq, w_out_hbm, w_query_hbm, w_key, w_value, outgoing, sent_ids,
    att_out, hid_out, enc_out, w_out, w_query, load_sem, returned, returned_ids,
    att_buf, hid_buf, enc_buf, att_first, hid_first, enc_first,
    att_send, att_recv, hid_send, hid_recv, enc_send, enc_recv,
    data_send, data_recv, ids_send, ids_recv, local_sem,
):
    me = lax.axis_index("dp")
    ahead, behind, chunk = ring_setup(n)
    rows = outgoing.shape[0] // owners
    width = att_out.shape[1]

    barrier = pltpu.get_barrier_semaphore()
    for device in [{"mp": ahead}, {"mp": behind}] + [{"dp": (me + d) % owners} for d in range(1, owners)]:
        pl.semaphore_signal(barrier, inc=1, device_id=device, device_id_type=pl.DeviceIdType.MESH)
    pl.semaphore_wait(barrier, 1 + owners)
    loads = [
        pltpu.make_async_copy(w_out_hbm, w_out, load_sem.at[0]),
        pltpu.make_async_copy(w_query_hbm, w_query, load_sem.at[1]),
    ]
    for load in loads:
        load.start()

    def block(index):
        return pl.ds(pl.multiple_of(index * rows, rows), rows)

    copies = []
    for d in range(1, owners):
        to = (me + d) % owners
        for src, dst, send, recv in (
            (outgoing.at[block(to)], returned.at[block(me)], data_send, data_recv),
            (sent_ids.at[to], returned_ids.at[me], ids_send, ids_recv),
        ):
            copies.append(pltpu.make_async_remote_copy(
                src_ref=src,
                dst_ref=dst,
                send_sem=send.at[d - 1],
                recv_sem=recv.at[d - 1],
                device_id={"dp": to},
                device_id_type=pl.DeviceIdType.MESH,
            ))
    local = [
        pltpu.make_async_copy(outgoing.at[block(me)], returned.at[block(me)], local_sem.at[0]),
        pltpu.make_async_copy(sent_ids.at[me], returned_ids.at[me], local_sem.at[1]),
    ]
    for copy in copies + local:
        copy.start()

    def at(index):
        return pl.ds(pl.multiple_of(index * width, width), width)

    tokens = returned.shape[1] // n
    window = max(tokens, 16)
    enc_rows = stored * tokens

    def enc_part(c):
        start = c * tokens
        base = pl.multiple_of(start // 16 * 16, 16)
        shape = (enc_rows, rows * window)
        row = lax.broadcasted_iota(jnp.int32, shape, 0)
        col = lax.broadcasted_iota(jnp.int32, shape, 1)
        same_token = col % window == start - base + row % tokens
        total = None
        for q in range(owners):
            slot = returned_ids[q, 0:1, 0:rows * window]
            hit = jnp.where(same_token & (slot == row // tokens), 1.0, 0.0).astype(jnp.bfloat16)
            block_rows = returned[q * rows:(q + 1) * rows, pl.ds(base, window), :]
            term = dot(hit, block_rows.reshape(rows * window, -1), (1, 0))
            total = term if total is None else total + term
        total = total.astype(jnp.bfloat16)
        cols = w_key.shape[1]
        return dot(total[:, :cols], w_key[...], (1, 1)) + dot(total[:, cols:], w_value[...], (1, 1))

    att = Ring(n, ahead, chunk, lambda c: dot(attn[...], w_out[:, at(c)], (1, 0)),
               att_buf, att_first, att_send, att_recv, att_out)
    hid = Ring(n, ahead, chunk, lambda c: dot(gq[...], w_query[at(c), :], (1, 1)),
               hid_buf, hid_first, hid_send, hid_recv, hid_out)
    enc = Ring(n, ahead, chunk, enc_part, enc_buf, enc_first, enc_send, enc_recv, enc_out)

    alone = n // 2 - 1
    loads[0].wait()
    att.first()
    loads[1].wait()
    hid.first()

    @pl.loop(1, alone + 1)
    def _(step):
        att.middle(step)
        hid.middle(step)

    att.middle(alone + 1)
    for copy in copies + local:
        copy.wait()
    enc.first()
    hid.middle(alone + 1)
    enc.middle(1)

    @pl.loop(alone + 2, n - 1)
    def _(step):
        done = 2 * (step - alone - 1)
        att.middle(step)
        enc.middle(done)
        hid.middle(step)
        enc.middle(done + 1)

    att.last()
    enc.middle(n - 2)
    hid.last()
    enc.last()
    for ring in (att, hid, enc):
        ring.drain()


def exchange(attn, gq, w_out, w_query, w_key, w_value, outgoing, sent_ids, stored):
    n, owners = lax.axis_size("mp"), lax.axis_size("dp")
    tok = attn.shape[0]
    width = w_out.shape[1] // n
    vmem = pl.BlockSpec(memory_space=pltpu.VMEM)
    anywhere = pl.BlockSpec(memory_space=pl.ANY)
    shapes = [(tok, width), (tok, width), (stored * outgoing.shape[1] // n, w_key.shape[0])]
    ring = pltpu.SemaphoreType.DMA((n - 1,))
    peers = pltpu.SemaphoreType.DMA((owners - 1,))
    return pl.pallas_call(
        functools.partial(exchange_kernel, n, owners, stored),
        in_specs=[vmem] * 2 + [anywhere] * 2 + [vmem] * 2 + [anywhere] * 2,
        out_specs=[vmem] * 3,
        out_shape=[jax.ShapeDtypeStruct(shape, jnp.bfloat16) for shape in shapes],
        scratch_shapes=[pltpu.VMEM(w.shape, w.dtype) for w in (w_out, w_query)]
        + [pltpu.SemaphoreType.DMA((2,))]
        + [pltpu.VMEM(outgoing.shape, outgoing.dtype), pltpu.VMEM(sent_ids.shape, sent_ids.dtype)]
        + [pltpu.VMEM((n - 1,) + shape, jnp.bfloat16) for shape in shapes]
        + [pltpu.VMEM(shape, jnp.bfloat16) for shape in shapes]
        + [ring] * 6
        + [peers] * 4
        + [pltpu.SemaphoreType.DMA((2,))],
        compiler_params=pltpu.CompilerParams(
            collective_id=1, has_side_effects=True, vmem_limit_bytes=VMEM_BYTES
        ),
        name="exchange",
    )(attn, gq, w_out, w_query, w_key, w_value, outgoing, sent_ids)


def fetch_kernel(
    nx, rows, hidden, w_query, cotangent, w_out, w_key, w_value, queries, grad_attn, kv,
    held, hid_v, wq_v, cot_v, wo_v,
    load_sem, x_send, x_recv, y_send, y_recv, own_send, own_recv,
    cx_send, cx_recv, cy_send, cy_recv,
):
    me, mp = lax.axis_index("dp"), lax.axis_index("mp")
    stored, seg, width = rows.shape
    half = stored // 2
    x, core, side = me // 2, me % 2, mp % 2
    twin = {"dp": x * 2 + 1 - core}
    pair = {"mp": mp + 1 - 2 * side}
    away = [{"dp": (x + d) % nx * 2 + core} for d in range(1, nx)]
    source = [(x - d + nx) % nx * 2 for d in range(1, nx)]

    barrier = pltpu.get_barrier_semaphore()
    for device in away + [twin, pair]:
        pl.semaphore_signal(barrier, inc=1, device_id=device, device_id_type=pl.DeviceIdType.MESH)
    pl.semaphore_wait(barrier, nx + 1)

    def send(src, place, sems, index, device):
        return pltpu.make_async_remote_copy(
            src_ref=src,
            dst_ref=held.at[place],
            send_sem=sems[0].at[index],
            recv_sem=sems[1].at[index],
            device_id=device,
            device_id_type=pl.DeviceIdType.MESH,
        )

    def relay(place, sems, index, device):
        return send(held.at[place], place, sems, index, device)

    steps = [(d, r) for r in range(half) for d in range(nx - 1)]
    mine, other = side * half, (1 - side) * half
    x_copies = [
        send(rows.at[mine + r], me * stored + mine + r, (x_send, x_recv), d * half + r, away[d])
        for d, r in steps
    ]
    own = send(rows, pl.ds(me * stored, stored), (own_send, own_recv), 0, twin)
    for copy in x_copies + [own]:
        copy.start()
    loads = [
        pltpu.make_async_copy(src, dst, load_sem.at[i])
        for i, (src, dst) in enumerate(((hidden, hid_v), (w_query, wq_v), (cotangent, cot_v), (w_out, wo_v)))
    ]
    for load in loads:
        load.start()

    def project(src, first, place):
        block = src[pl.ds(first, half)].reshape(half * seg, width)
        cols = w_key.shape[1]
        keys = dot(block, w_key[...], (1, 0)).astype(jnp.bfloat16)
        kv[pl.ds(place, half), :, :cols] = keys.reshape(half, seg, -1)
        values = dot(block, w_value[...], (1, 0)).astype(jnp.bfloat16)
        kv[pl.ds(place, half), :, cols:] = values.reshape(half, seg, -1)

    y_copies, cx_copies, cy_copies = [], [], []

    def pass_on(at):
        d, r = steps[at]
        place = (source[d] + core) * stored + mine + r
        x_copies[at].wait_recv()
        y_copies.append(relay(place, (y_send, y_recv), d * half + r, pair))
        cx_copies.append(relay(place, (cx_send, cx_recv), d * half + r, twin))
        y_copies[-1].start()
        cx_copies[-1].start()

    def finish(at):
        d, r = steps[at]
        place = (source[d] + core) * stored + other + r
        y_copies[at].wait_recv()
        cy_copies.append(relay(place, (cy_send, cy_recv), d * half + r, twin))
        cy_copies[-1].start()

    @pl.loop(0, 2)
    def _(i):
        project(rows, i * half, me * stored + i * half)

    quarter = len(steps) // 4
    pass_next = 0
    for _ in range(quarter):
        pass_on(pass_next)
        pass_next += 1
    loads[0].wait()
    loads[1].wait()
    queries[...] = dot(hid_v[...], wq_v[...], (1, 0)).astype(jnp.bfloat16)
    for _ in range(quarter):
        pass_on(pass_next)
        pass_next += 1
    loads[2].wait()
    loads[3].wait()
    grad_attn[...] = dot(cot_v[...], wo_v[...], (1, 1)).astype(jnp.bfloat16)
    for _ in range(quarter):
        pass_on(pass_next)
        pass_next += 1
    own.wait_recv()

    @pl.loop(0, 2)
    def _(i):
        first = (x * 2 + 1 - core) * stored + i * half
        project(held, first, first)

    while pass_next < len(steps):
        pass_on(pass_next)
        pass_next += 1
    early = max(len(steps) - nx + 1, 0)
    for at in range(early):
        finish(at)
    for copy in cx_copies:
        copy.wait_recv()

    def project_all(first):
        for d in range(nx - 1):
            @pl.loop(0, 2)
            def _(i):
                place = (source[d] + i) * stored + first
                project(held, place, place)

    project_all(mine)
    for at in range(early, len(steps)):
        finish(at)
    for copy in cy_copies:
        copy.wait_recv()
    project_all(other)
    for copy in x_copies + [own] + y_copies + cx_copies + cy_copies:
        copy.wait_send()


def fetch(rows, hidden, w_query, cotangent, w_out, w_key, w_value):
    owners = lax.axis_size("dp")
    nx = owners // 2
    stored, seg, _ = rows.shape
    vmem = pl.BlockSpec(memory_space=pltpu.VMEM)
    anywhere = pl.BlockSpec(memory_space=pl.ANY)
    tok, cols = hidden.shape[0], w_query.shape[1]
    pieces = pltpu.SemaphoreType.DMA(((nx - 1) * stored // 2,))
    return pl.pallas_call(
        functools.partial(fetch_kernel, nx),
        in_specs=[vmem] + [anywhere] * 4 + [vmem] * 2,
        out_specs=[vmem] * 3,
        out_shape=[
            jax.ShapeDtypeStruct((tok, cols), jnp.bfloat16),
            jax.ShapeDtypeStruct((tok, cols), jnp.bfloat16),
            jax.ShapeDtypeStruct((owners * stored, seg, 2 * w_key.shape[1]), jnp.bfloat16),
        ],
        scratch_shapes=[pltpu.VMEM((owners * stored,) + rows.shape[1:], jnp.bfloat16)]
        + [pltpu.VMEM(a.shape, a.dtype) for a in (hidden, w_query, cotangent, w_out)]
        + [pltpu.SemaphoreType.DMA((4,))]
        + [pieces] * 4
        + [pltpu.SemaphoreType.DMA((1,))] * 2
        + [pieces] * 4,
        compiler_params=pltpu.CompilerParams(
            collective_id=3, has_side_effects=True, vmem_limit_bytes=VMEM_BYTES
        ),
        name="fetch",
    )(rows, hidden, w_query, cotangent, w_out, w_key, w_value)


def shards(hidden, encoded, neighbours, w_query, w_key, w_value, w_out, cotangent):
    owners = lax.axis_size("dp")
    blocks, per_block = neighbours.shape
    requests = blocks * per_block
    capacity = requests // 4
    stored = encoded.shape[0]
    enc_width, head_cols = w_key.shape
    seg_len = encoded.shape[1] // enc_width

    queries, grad_attn, kv = fetch(
        encoded.reshape(stored, seg_len, enc_width), hidden, w_query, cotangent, w_out, w_key, w_value
    )
    flat_ids = neighbours.reshape(requests)
    flat_owner = flat_ids // stored
    mine = flat_owner[:, None] == flat_owner[None, :]
    before = jnp.arange(requests)[:, None] > jnp.arange(requests)[None, :]
    target = flat_owner * capacity + jnp.sum((mine & before).astype(jnp.int32), axis=1)
    placed = target[:, None] == jnp.arange(owners * capacity)[None, :]
    sent_ids = jnp.sum(jnp.where(placed, (flat_ids % stored)[:, None] + 1, 0), axis=0) - 1
    parts = lax.axis_size("mp")
    window = max(seg_len // parts, 16)
    sent_ids = jnp.repeat(sent_ids.reshape(owners, 1, capacity), window, axis=2)
    pad = -capacity * window % 128
    sent_ids = jnp.pad(jnp.broadcast_to(sent_ids, (owners, 8, capacity * window)), ((0, 0), (0, 0), (0, pad)))

    attn, grad_query, outgoing = attention(
        flat_ids, target, queries, grad_attn, kv, blocks, owners * capacity
    )
    attended, grad_hidden, grad_encoded = exchange(
        attn, grad_query, w_out, w_query, w_key, w_value, outgoing, sent_ids, stored
    )
    return attended, grad_hidden, grad_encoded.reshape(stored, -1)


def solution(mesh):
    placed = (
        P("dp", None),
        P("dp", None),
        P("dp", None),
        P(None, "mp"),
        P(None, "mp"),
        P(None, "mp"),
        P("mp", None),
        P("dp", None),
    )
    return jax.shard_map(
        shards,
        mesh=mesh,
        in_specs=placed,
        out_specs=(P("dp", "mp"), P("dp", "mp"), P("dp", "mp")),
        check_vma=False,
    )
```
